32 devices in a mesh: rep: 16 (over z, x, core), fsdp: 2 (over y).
Axes of the slice: x: 2, y: 2, z: 4, core: 2. Of those that a mesh axis runs over, the one named last changes fastest.
Arguments:
- numerator: bfloat16 [16, 2560, 2560], P('rep', None, 'fsdp'), may hold values from -6 to 6
- push_weight: float32 [16], P('rep'), may hold values from 0.5 to 2
- norm_gain: float32 [2560], replicated, may hold values from 0.1 to 1.9
- activations: bfloat16 [2, 2816, 2560], P(None, ('rep', 'fsdp')), may hold values from -40 to 40, as said below
- cotangent: bfloat16 [2, 2816, 2560], P(None, ('rep', 'fsdp')), may hold values from -6 to 6
- step_index: int32 [], replicated, may hold values from 0 to 999
Outputs:
- mixed: bfloat16 [16, 2560, 2560], P('rep', None, 'fsdp')
- new_weight: float32 [16], P('rep')
The draws below stay inside these ranges and needn't reach their ends.
Inputs may be any that keep to these rules, and one draw needn't show every extreme that they name: `activations`: Per-token and per-feature scales vary.
All inputs are finite; a program needn't handle non-finite values.
Results may differ from the reference program's by a relative error of at most 0.0075.
Values may be sent and summed in bfloat16 or wider, within the bound.
A program may use at most 128 MiB of HBM per device.

```python
import math
import jax
import jax.numpy as jnp
from jax import lax

DW = 2560
HW = 2560
MICRO = 2
MB_DEV = 88
TOKENS_MB = 2816
N_REP = 16
N_FSDP = 2


def draw_activations(key, part):
    key = jax.random.fold_in(key, 11)
    k_base, k_rows, k_cols = jax.random.split(key, 3)
    row_scale = jnp.exp(jax.random.uniform(k_rows, (MICRO, TOKENS_MB, 1), jnp.float32, jnp.log(0.3), jnp.log(3.0)))
    col_scale = jnp.exp(jax.random.uniform(k_cols, (1, 1, DW), jnp.float32, jnp.log(0.3), jnp.log(3.0)))
    base = jnp.clip(jax.random.normal(k_base, (MICRO, TOKENS_MB, DW), jnp.float32), -4.0, 4.0)
    return (base * row_scale * col_scale).astype(jnp.bfloat16)


def shard_levels(key, dims, cuts, smallest, high):
    def one(axis_at, shards_of):
        draws = jax.random.uniform(jax.random.fold_in(jax.random.fold_in(key, 6), axis_at), (shards_of,), jnp.float32, smallest / len(cuts), high / len(cuts))
        return jnp.repeat(jnp.exp(draws), dims[axis_at] // shards_of).reshape((-1,) + (1,) * (len(dims) - axis_at - 1))

    factor_of = one(*cuts[0])
    for cut in cuts[1:]:
        factor_of = factor_of * one(*cut)
    return factor_of


def bell_draw(stream_key, shape, scale, most, shards=(), kind=jnp.bfloat16):
    level = shard_levels(stream_key, shape, shards, -0.22, 0.18) if shards else 1.0
    values = jax.random.normal(stream_key, shape, jnp.float32) * scale * level
    return jnp.minimum(jnp.maximum(values, -most), most).astype(kind)


def setup_inputs(seed: int = 0) -> dict:
    keys = jax.random.split(jax.random.key(seed), 7)
    return {
        "numerator": bell_draw(keys[0], (N_REP, DW, HW), 1.0, 6.0, ((0, 16), (2, 2))),
        "push_weight": jnp.clip(jnp.exp(math.log(2.0) - 1.3862944 * jax.random.uniform(keys[1], (N_REP,), jnp.float32) ** shard_levels(keys[1], (N_REP,), ((0, 16),), -0.2, 0.2)), 0.5, 2.0),
        "norm_gain": jnp.clip(1.0 + 0.18 * jax.random.normal(keys[2], (DW,), jnp.float32), 0.1, 1.9),
        "activations": draw_activations(jax.random.fold_in(keys[6], 71), 0),
        "cotangent": bell_draw(keys[4], (MICRO, TOKENS_MB, HW), 1.0, 6.0, ((1, 32),)),
        "step_index": jax.random.randint(keys[5], (), 0, 1000).astype(jnp.int32),
    }


LEARN_RATE = 1.5
EPSILON = 1e-05

def silu_slope(pre_act):
    sig = jax.nn.sigmoid(pre_act)
    return sig * (1.0 + pre_act * (1.0 - sig))

def reference(numerator, push_weight, norm_gain, activations, cotangent, step_index):
    group = MB_DEV * N_FSDP
    scale = DW ** (-0.5)
    acts = activations.reshape(MICRO, N_REP, group, DW).transpose(1, 0, 2, 3).reshape(N_REP, MICRO * group, DW)
    cots = cotangent.reshape(MICRO, N_REP, group, HW).transpose(1, 0, 2, 3).reshape(N_REP, MICRO * group, HW)

    def one_replica(items):
        inputs, cot_rows, numer, weight = items
        wide = inputs.astype(jnp.float32)
        mean_square = lax.optimization_barrier(jnp.mean(wide * wide, axis=-1, keepdims=True))
        normed = (wide * lax.rsqrt(mean_square + EPSILON) * norm_gain).astype(jnp.bfloat16)
        eff_weight = (numer.astype(jnp.float32) / weight).astype(jnp.bfloat16)
        pre_act = scale * jnp.dot(normed, eff_weight, preferred_element_type=jnp.float32)
        grad_out = (cot_rows.astype(jnp.float32) * silu_slope(pre_act)).astype(jnp.bfloat16)
        grad = scale * jnp.dot(normed.T, grad_out, preferred_element_type=jnp.float32)
        return (LEARN_RATE * grad).astype(jnp.bfloat16)
    updates = lax.map(one_replica, (acts, cots, numerator, push_weight))
    bit_count = N_REP.bit_length() - 1
    hop_size = jnp.left_shift(jnp.int32(1), (step_index % bit_count).astype(jnp.int32))
    source = ((jnp.arange(N_REP, dtype=jnp.int32) - hop_size) % N_REP).astype(jnp.int32)
    local = numerator.astype(jnp.float32) - updates.astype(jnp.float32)
    mixed = (0.5 * local + 0.5 * local[source]).astype(jnp.bfloat16)
    new_weight = 0.5 * (push_weight + push_weight[source])
    return (mixed, new_weight)
```

```python
from functools import partial

import jax
import jax.numpy as jnp
from jax import lax
from jax.sharding import PartitionSpec as P

LEARN_RATE = 1.5
EPSILON = 1e-05
PIECES = 4


def shifted(block, axis, distance):
    count = lax.axis_size(axis)
    route = [((i - distance) % count, i) for i in range(count)]
    return lax.ppermute(block, axis, route)


def silu_slope(pre_act):
    sig = jax.nn.sigmoid(pre_act)
    return sig * (1.0 + pre_act * (1.0 - sig))


def normalised(activations, norm_gain):
    wide = activations.astype(jnp.float32)
    mean_square = jnp.mean(wide * wide, axis=-1, keepdims=True)
    return (wide * lax.rsqrt(mean_square + EPSILON) * norm_gain).astype(jnp.bfloat16)


def token_rows(activations, cotangent):
    count = lax.axis_size("fsdp")
    me = lax.axis_index("fsdp")
    width = cotangent.shape[2] // count
    acts, cots = [activations], [lax.dynamic_slice_in_dim(cotangent, me * width, width, 2)]
    for step in range(1, count):
        acts.append(shifted(activations, "fsdp", step))
        theirs = lax.rem(me + step, count)
        cots.append(shifted(lax.dynamic_slice_in_dim(cotangent, theirs * width, width, 2), "fsdp", step))
    return jnp.concatenate(acts, axis=1), jnp.concatenate(cots, axis=1)


def mix(state, hop_size):
    numerator, push_weight, normed, grad_out = state
    depth = numerator.shape[0]
    scale = depth ** (-0.5)
    rows = depth // PIECES
    mixed = []
    partner_weight = shifted(push_weight, "rep", hop_size)
    for start in range(0, depth, rows):
        grad = scale * jnp.einsum(
            "td,th->dh", normed[:, start : start + rows], grad_out, preferred_element_type=jnp.float32
        )
        update = (LEARN_RATE * grad).astype(jnp.bfloat16).astype(jnp.float32)
        local = (numerator[start : start + rows].astype(jnp.float32) - update).astype(jnp.bfloat16)
        theirs = shifted(local, "rep", hop_size)
        mixed.append((0.5 * (local.astype(jnp.float32) + theirs.astype(jnp.float32))).astype(jnp.bfloat16))
    return jnp.concatenate(mixed, axis=0), 0.5 * (push_weight + partner_weight)


def on_device(numerator, push_weight, norm_gain, activations, cotangent, step_index):
    acts, cots = token_rows(activations, cotangent)
    depth, width = numerator.shape[1:]
    scale = depth ** (-0.5)
    normed = normalised(acts, norm_gain).reshape(-1, depth)
    cots = cots.reshape(-1, width)
    eff_weight = (numerator[0].astype(jnp.float32) / push_weight[0]).astype(jnp.bfloat16)
    pre_act = scale * jnp.dot(normed, eff_weight, preferred_element_type=jnp.float32)
    grad_out = (cots.astype(jnp.float32) * silu_slope(pre_act)).astype(jnp.bfloat16)
    bit_count = lax.axis_size("rep").bit_length() - 1
    branches = [partial(mix, hop_size=2**bit) for bit in range(bit_count)]
    mixed, new_weight = lax.switch(
        step_index % bit_count, branches, (numerator[0], push_weight, normed, grad_out)
    )
    return mixed[None], new_weight


def solution(mesh):
    placed = (
        P("rep", None, "fsdp"),
        P("rep"),
        P(),
        P(None, ("rep", "fsdp"), None),
        P(None, ("rep", "fsdp"), None),
        P(),
    )
    return jax.shard_map(
        on_device,
        mesh=mesh,
        in_specs=placed,
        out_specs=(P("rep", None, "fsdp"), P("rep")),
        check_vma=False,
    )
```

```python
from functools import partial

import jax
import jax.numpy as jnp
from jax import lax
from jax.experimental import pallas as pl
from jax.experimental.pallas import tpu as pltpu
from jax.sharding import PartitionSpec as P

LEARN_RATE = 1.5
EPSILON = 1e-05
PIECES = 4
CHUNK = 256
BLOCK = 512
ROWS = 16
MESH = pl.DeviceIdType.MESH


def shifted(block, axis, distance):
    count = lax.axis_size(axis)
    route = [((i - distance) % count, i) for i in range(count)]
    return lax.ppermute(block, axis, route)


def silu_slope(pre_act):
    sig = jax.nn.sigmoid(pre_act)
    return sig * (1.0 + pre_act * (1.0 - sig))


def normalised(activations, norm_gain):
    wide = activations.astype(jnp.float32)
    mean_square = jnp.mean(wide * wide, axis=-1, keepdims=True)
    return (wide * lax.rsqrt(mean_square + EPSILON) * norm_gain).astype(jnp.bfloat16)


def token_rows(activations, cotangent):
    count = lax.axis_size("fsdp")
    me = lax.axis_index("fsdp")
    width = cotangent.shape[2] // count
    acts, cots = [activations], [lax.dynamic_slice_in_dim(cotangent, me * width, width, 2)]
    for step in range(1, count):
        acts.append(shifted(activations, "fsdp", step))
        theirs = lax.rem(me + step, count)
        cots.append(shifted(lax.dynamic_slice_in_dim(cotangent, theirs * width, width, 2), "fsdp", step))
    return jnp.concatenate(acts, axis=1), jnp.concatenate(cots, axis=1)


def mix(state, hop_size):
    numerator, push_weight, normed, grad_out = state
    depth = numerator.shape[0]
    scale = depth ** (-0.5)
    rows = depth // PIECES
    mixed = []
    partner_weight = shifted(push_weight, "rep", hop_size)
    for start in range(0, depth, rows):
        grad = scale * jnp.einsum(
            "td,th->dh", normed[:, start : start + rows], grad_out, preferred_element_type=jnp.float32
        )
        update = (LEARN_RATE * grad).astype(jnp.bfloat16).astype(jnp.float32)
        local = (numerator[start : start + rows].astype(jnp.float32) - update).astype(jnp.bfloat16)
        theirs = shifted(local, "rep", hop_size)
        mixed.append((0.5 * (local.astype(jnp.float32) + theirs.astype(jnp.float32))).astype(jnp.bfloat16))
    return jnp.concatenate(mixed, axis=0), 0.5 * (push_weight + partner_weight)


def on_device(numerator, push_weight, norm_gain, activations, cotangent, step_index):
    acts, cots = token_rows(activations, cotangent)
    depth, width = numerator.shape[1:]
    scale = depth ** (-0.5)
    normed = normalised(acts, norm_gain).reshape(-1, depth)
    cots = cots.reshape(-1, width)
    eff_weight = (numerator[0].astype(jnp.float32) / push_weight[0]).astype(jnp.bfloat16)
    pre_act = scale * jnp.dot(normed, eff_weight, preferred_element_type=jnp.float32)
    grad_out = (cots.astype(jnp.float32) * silu_slope(pre_act)).astype(jnp.bfloat16)
    bit_count = lax.axis_size("rep").bit_length() - 1
    branches = [partial(mix, hop_size=2**bit) for bit in range(bit_count)]
    mixed, new_weight = lax.switch(
        step_index % bit_count, branches, (numerator[0], push_weight, normed, grad_out)
    )
    return mixed[None], new_weight


def push_kernel(
    hop_size, weight_ref, gain_ref, numer_hbm, act_hbm, cot_hbm, mixed_hbm, new_weight_ref,
    act_v, cot_v, normed_v, pre_v, grad_v, local_v, theirs_v, weight_v,
    load_sem, act_sem, act_send, act_recv, cot_sem, cot_send, cot_recv,
    state_send, state_recv, weight_send, weight_recv, out_sem,
):
    rep, col = lax.axis_index("rep"), lax.axis_index("fsdp")
    n_rep = lax.axis_size("rep")
    mate = (rep, 1 - col)
    target = (lax.rem(rep + hop_size, n_rep), col)
    source = (lax.rem(rep + n_rep - hop_size, n_rep), col)
    tokens, depth = act_hbm.shape
    chunks, _, chunk = local_v.shape
    width = chunks * chunk
    scale = depth ** (-0.5)
    cut = tokens // 2 // ROWS * ROWS
    halves = ((0, cut), (cut, tokens - cut))

    def load(c):
        columns = pl.ds(pl.multiple_of(c * chunk, chunk), chunk)
        return pltpu.make_async_copy(numer_hbm.at[:, columns], local_v.at[c], load_sem.at[c])

    def own_cot(c):
        columns = pl.ds(pl.multiple_of(col * width + c * chunk, chunk), chunk)
        return pltpu.make_async_copy(cot_hbm.at[:, columns], cot_v.at[0, c], cot_sem.at[c])

    def send_cot(c):
        columns = pl.ds(pl.multiple_of((1 - col) * width + c * chunk, chunk), chunk)
        return pltpu.make_async_remote_copy(
            src_ref=cot_hbm.at[:, columns], dst_ref=cot_v.at[1, c],
            send_sem=cot_send.at[c], recv_sem=cot_recv.at[c], device_id=mate, device_id_type=MESH,
        )

    def send_act(i):
        rows = pl.ds(*halves[i])
        return pltpu.make_async_remote_copy(
            src_ref=act_hbm.at[rows], dst_ref=act_v.at[1, rows],
            send_sem=act_send.at[i], recv_sem=act_recv.at[i], device_id=mate, device_id_type=MESH,
        )

    def send_state(c):
        return pltpu.make_async_remote_copy(
            src_ref=local_v.at[c], dst_ref=theirs_v.at[c],
            send_sem=state_send.at[c], recv_sem=state_recv.at[c], device_id=target, device_id_type=MESH,
        )

    def store(c):
        columns = pl.ds(pl.multiple_of(c * chunk, chunk), chunk)
        return pltpu.make_async_copy(theirs_v.at[c], mixed_hbm.at[:, columns], out_sem.at[c])

    send_weight = pltpu.make_async_remote_copy(
        src_ref=weight_ref, dst_ref=weight_v,
        send_sem=weight_send, recv_sem=weight_recv, device_id=target, device_id_type=MESH,
    )
    own_act = pltpu.make_async_copy(act_hbm, act_v.at[0], act_sem)

    barrier = pltpu.get_barrier_semaphore()
    for device in (mate, source):
        pl.semaphore_signal(barrier, inc=1, device_id=device, device_id_type=MESH)
    own_act.start()
    pl.semaphore_wait(barrier, 2)
    send_act(0).start()
    send_act(1).start()
    send_cot(0).start()
    send_weight.start()
    for c in range(chunks):
        own_cot(c).start()
        load(c).start()

    gain = gain_ref[...]

    def normalise(side, first, count):
        @pl.loop(0, count // ROWS)
        def _(i):
            rows = pl.ds(pl.multiple_of(first + i * ROWS, ROWS), ROWS)
            wide = act_v[side, rows, :].astype(jnp.float32)
            mean_square = jnp.mean(wide * wide, axis=-1, keepdims=True)
            normed = wide * lax.rsqrt(mean_square + EPSILON) * gain
            normed_v[pl.ds(pl.multiple_of(side * tokens + first + i * ROWS, ROWS), ROWS), :] = normed.astype(jnp.bfloat16)

    own_act.wait()
    normalise(0, 0, tokens)
    send_act(0).wait_recv()
    normalise(1, *halves[0])
    send_act(1).wait_recv()
    for c in range(1, chunks):
        send_cot(c).start()
    normalise(1, *halves[1])

    inverse = 1.0 / weight_ref[0:1, :]

    @pl.loop(0, chunks)
    def _(c):
        load(c).wait()
        pre_v[...] = jnp.zeros_like(pre_v)

        @pl.loop(0, depth // BLOCK)
        def _(k):
            part = pl.ds(pl.multiple_of(k * BLOCK, BLOCK), BLOCK)
            eff_weight = (local_v[c, part, :].astype(jnp.float32) * inverse).astype(jnp.bfloat16)
            pre_v[...] += jnp.dot(normed_v[:, part], eff_weight, preferred_element_type=jnp.float32)

        own_cot(c).wait()
        send_cot(c).wait_recv()
        for side in range(2):
            rows = pl.ds(side * tokens, tokens)
            grad_v[rows, :] = (
                cot_v[side, c].astype(jnp.float32) * silu_slope(scale * pre_v[rows, :])
            ).astype(jnp.bfloat16)

        @pl.loop(0, depth // BLOCK)
        def _(k):
            part = pl.ds(pl.multiple_of(k * BLOCK, BLOCK), BLOCK)
            grad = lax.dot_general(
                normed_v[:, part], grad_v[...], (((0,), (0,)), ((), ())), preferred_element_type=jnp.float32
            )
            update = (LEARN_RATE * (scale * grad)).astype(jnp.bfloat16).astype(jnp.float32)
            local_v[c, part, :] = (local_v[c, part, :].astype(jnp.float32) - update).astype(jnp.bfloat16)

        send_state(c).start()

    send_weight.wait_recv()
    new_weight_ref[...] = 0.5 * (weight_ref[...] + weight_v[...])

    @pl.loop(0, chunks)
    def _(c):
        send_state(c).wait_recv()

        @pl.loop(0, depth // BLOCK)
        def _(k):
            part = pl.ds(pl.multiple_of(k * BLOCK, BLOCK), BLOCK)
            both = local_v[c, part, :].astype(jnp.float32) + theirs_v[c, part, :].astype(jnp.float32)
            theirs_v[c, part, :] = (0.5 * both).astype(jnp.bfloat16)

        store(c).start()

    send_act(0).wait_send()
    send_act(1).wait_send()
    send_weight.wait_send()

    @pl.loop(0, chunks)
    def _(c):
        send_cot(c).wait_send()
        send_state(c).wait_send()
        store(c).wait()


def push(state, hop_size, collective_id):
    numerator, push_weight, norm_gain, activations, cotangent = state
    depth, width = numerator.shape
    tokens = activations.shape[0]
    chunks = width // CHUNK
    vmem, hbm = pl.BlockSpec(memory_space=pltpu.VMEM), pl.BlockSpec(memory_space=pl.ANY)
    weight = jnp.broadcast_to(push_weight[:, None], (8, CHUNK))
    dma = pltpu.SemaphoreType.DMA
    mixed, new_weight = pl.pallas_call(
        partial(push_kernel, hop_size),
        out_shape=(
            jax.ShapeDtypeStruct((depth, width), jnp.bfloat16),
            jax.ShapeDtypeStruct((8, CHUNK), jnp.float32),
        ),
        in_specs=[vmem, vmem, hbm, hbm, hbm],
        out_specs=(hbm, vmem),
        scratch_shapes=[
            pltpu.VMEM((2, tokens, depth), jnp.bfloat16),
            pltpu.VMEM((2, chunks, tokens, CHUNK), jnp.bfloat16),
            pltpu.VMEM((2 * tokens, depth), jnp.bfloat16),
            pltpu.VMEM((2 * tokens, CHUNK), jnp.float32),
            pltpu.VMEM((2 * tokens, CHUNK), jnp.bfloat16),
            pltpu.VMEM((chunks, depth, CHUNK), jnp.bfloat16),
            pltpu.VMEM((chunks, depth, CHUNK), jnp.bfloat16),
            pltpu.VMEM((8, CHUNK), jnp.float32),
            dma((chunks,)), dma, dma((2,)), dma((2,)), dma((chunks,)), dma((chunks,)), dma((chunks,)),
            dma((chunks,)), dma((chunks,)), dma, dma, dma((chunks,)),
        ],
        compiler_params=pltpu.CompilerParams(
            collective_id=collective_id, has_side_effects=True, vmem_limit_bytes=48 * 2**20
        ),
        cost_estimate=pl.CostEstimate(
            flops=8 * tokens * depth * width, bytes_accessed=4 * depth * width, transcendentals=2 * tokens * width
        ),
    )(weight, norm_gain[None], numerator, activations, cotangent)
    return mixed, new_weight[0, :1]


def on_pairs(numerator, push_weight, norm_gain, activations, cotangent, step_index):
    depth = numerator.shape[1]
    state = (
        numerator[0], push_weight, norm_gain,
        activations.reshape(-1, depth), cotangent.reshape(-1, cotangent.shape[2]),
    )
    bit_count = lax.axis_size("rep").bit_length() - 1
    branches = [partial(push, hop_size=2**bit, collective_id=bit) for bit in range(bit_count)]
    mixed, new_weight = lax.switch(step_index % bit_count, branches, state)
    return mixed[None], new_weight


def solution(mesh):
    placed = (
        P("rep", None, "fsdp"),
        P("rep"),
        P(),
        P(None, ("rep", "fsdp"), None),
        P(None, ("rep", "fsdp"), None),
        P(),
    )
    return jax.shard_map(
        on_pairs if mesh.shape["fsdp"] == 2 else on_device,
        mesh=mesh,
        in_specs=placed,
        out_specs=(P("rep", None, "fsdp"), P("rep")),
        check_vma=False,
    )
```

```python
from functools import partial

import jax
import jax.numpy as jnp
from jax import lax
from jax.experimental import pallas as pl
from jax.experimental.pallas import tpu as pltpu
from jax.sharding import PartitionSpec as P

LEARN_RATE = 1.5
EPSILON = 1e-05
PIECES = 4
CHUNK = 256
BLOCK = 512
ROWS = 16
PIECE = 48
MESH = pl.DeviceIdType.MESH


def shifted(block, axis, distance):
    count = lax.axis_size(axis)
    route = [((i - distance) % count, i) for i in range(count)]
    return lax.ppermute(block, axis, route)


def silu_slope(pre_act):
    sig = jax.nn.sigmoid(pre_act)
    return sig * (1.0 + pre_act * (1.0 - sig))


def normalised(activations, norm_gain):
    wide = activations.astype(jnp.float32)
    mean_square = jnp.mean(wide * wide, axis=-1, keepdims=True)
    return (wide * lax.rsqrt(mean_square + EPSILON) * norm_gain).astype(jnp.bfloat16)


def token_rows(activations, cotangent):
    count = lax.axis_size("fsdp")
    me = lax.axis_index("fsdp")
    width = cotangent.shape[2] // count
    acts, cots = [activations], [lax.dynamic_slice_in_dim(cotangent, me * width, width, 2)]
    for step in range(1, count):
        acts.append(shifted(activations, "fsdp", step))
        theirs = lax.rem(me + step, count)
        cots.append(shifted(lax.dynamic_slice_in_dim(cotangent, theirs * width, width, 2), "fsdp", step))
    return jnp.concatenate(acts, axis=1), jnp.concatenate(cots, axis=1)


def mix(state, hop_size):
    numerator, push_weight, normed, grad_out = state
    depth = numerator.shape[0]
    scale = depth ** (-0.5)
    rows = depth // PIECES
    mixed = []
    partner_weight = shifted(push_weight, "rep", hop_size)
    for start in range(0, depth, rows):
        grad = scale * jnp.einsum(
            "td,th->dh", normed[:, start : start + rows], grad_out, preferred_element_type=jnp.float32
        )
        update = (LEARN_RATE * grad).astype(jnp.bfloat16).astype(jnp.float32)
        local = (numerator[start : start + rows].astype(jnp.float32) - update).astype(jnp.bfloat16)
        theirs = shifted(local, "rep", hop_size)
        mixed.append((0.5 * (local.astype(jnp.float32) + theirs.astype(jnp.float32))).astype(jnp.bfloat16))
    return jnp.concatenate(mixed, axis=0), 0.5 * (push_weight + partner_weight)


def on_device(numerator, push_weight, norm_gain, activations, cotangent, step_index):
    acts, cots = token_rows(activations, cotangent)
    depth, width = numerator.shape[1:]
    scale = depth ** (-0.5)
    normed = normalised(acts, norm_gain).reshape(-1, depth)
    cots = cots.reshape(-1, width)
    eff_weight = (numerator[0].astype(jnp.float32) / push_weight[0]).astype(jnp.bfloat16)
    pre_act = scale * jnp.dot(normed, eff_weight, preferred_element_type=jnp.float32)
    grad_out = (cots.astype(jnp.float32) * silu_slope(pre_act)).astype(jnp.bfloat16)
    bit_count = lax.axis_size("rep").bit_length() - 1
    branches = [partial(mix, hop_size=2**bit) for bit in range(bit_count)]
    mixed, new_weight = lax.switch(
        step_index % bit_count, branches, (numerator[0], push_weight, normed, grad_out)
    )
    return mixed[None], new_weight


def push_kernel(
    hop_size, weight_ref, gain_ref, numer_hbm, act_hbm, cot_hbm, mixed_hbm, new_weight_ref,
    act_v, cot_v, normed_v, pre_v, grad_v, local_v, theirs_v, weight_v,
    load_sem, act_sem, act_send, act_recv, cot_sem, cot_send, cot_recv,
    state_send, state_recv, weight_send, weight_recv, out_sem, go_sem,
):
    rep, col = lax.axis_index("rep"), lax.axis_index("fsdp")
    n_rep = lax.axis_size("rep")
    mate = (rep, 1 - col)
    target = (lax.rem(rep + hop_size, n_rep), col)
    source = (lax.rem(rep + n_rep - hop_size, n_rep), col)
    odd = lax.rem(rep, 2)
    sibling = (rep + 1 - 2 * odd, col)
    leads = odd == (1 if hop_size == 1 else 0)
    tokens, depth = act_hbm.shape
    chunks, _, chunk = local_v.shape
    blocks = depth // BLOCK
    width = chunks * chunk
    scale = depth ** (-0.5)
    pieces = [(first, min(PIECE, tokens - first)) for first in range(0, tokens, PIECE)]

    def columns_of(c):
        return pl.ds(pl.multiple_of(c * chunk, chunk), chunk)

    def block_of(k):
        return pl.ds(pl.multiple_of(k * BLOCK, BLOCK), BLOCK)

    def load(c):
        return pltpu.make_async_copy(numer_hbm.at[:, columns_of(c)], local_v.at[c], load_sem.at[c])

    def own_cot(c):
        columns = pl.ds(pl.multiple_of(col * width + c * chunk, chunk), chunk)
        return pltpu.make_async_copy(cot_hbm.at[:, columns], cot_v.at[0, c], cot_sem.at[c])

    def send_cot(c):
        columns = pl.ds(pl.multiple_of((1 - col) * width + c * chunk, chunk), chunk)
        return pltpu.make_async_remote_copy(
            src_ref=cot_hbm.at[:, columns], dst_ref=cot_v.at[1, c],
            send_sem=cot_send.at[c], recv_sem=cot_recv.at[c], device_id=mate, device_id_type=MESH,
        )

    def send_act(i):
        rows = pl.ds(*pieces[i])
        return pltpu.make_async_remote_copy(
            src_ref=act_hbm.at[rows], dst_ref=act_v.at[1, rows],
            send_sem=act_send.at[i], recv_sem=act_recv.at[i], device_id=mate, device_id_type=MESH,
        )

    def send_state(c, k):
        return pltpu.make_async_remote_copy(
            src_ref=local_v.at[c, block_of(k)], dst_ref=theirs_v.at[c, block_of(k)],
            send_sem=state_send.at[c, k], recv_sem=state_recv.at[c, k], device_id=target, device_id_type=MESH,
        )

    def store(c, k):
        return pltpu.make_async_copy(
            theirs_v.at[c, block_of(k)], mixed_hbm.at[block_of(k), columns_of(c)], out_sem.at[c, k]
        )

    def start_sends():
        for i in range(len(pieces)):
            send_act(i).start()
        send_cot(0).start()

    send_weight = pltpu.make_async_remote_copy(
        src_ref=weight_v.at[0], dst_ref=weight_v.at[1],
        send_sem=weight_send, recv_sem=weight_recv, device_id=target, device_id_type=MESH,
    )
    own_act = pltpu.make_async_copy(act_hbm, act_v.at[0], act_sem)

    barrier = pltpu.get_barrier_semaphore()
    for device in (mate, source, sibling):
        pl.semaphore_signal(barrier, inc=1, device_id=device, device_id_type=MESH)
    own_act.start()
    weight_v[0] = jnp.full(weight_v.shape[1:], weight_ref[0], jnp.float32)
    pl.semaphore_wait(barrier, 3)

    @pl.when(leads)
    def _():
        start_sends()

    send_weight.start()
    for c in range(chunks):
        own_cot(c).start()
        load(c).start()

    gain = gain_ref[...].reshape(1, depth)

    def normalise(side, first, count):
        @pl.loop(0, count // ROWS)
        def _(i):
            rows = pl.ds(pl.multiple_of(first + i * ROWS, ROWS), ROWS)
            wide = act_v[side, rows, :].astype(jnp.float32)
            mean_square = jnp.mean(wide * wide, axis=-1, keepdims=True)
            normed = wide * lax.rsqrt(mean_square + EPSILON) * gain
            normed_v[pl.ds(pl.multiple_of(side * tokens + first + i * ROWS, ROWS), ROWS), :] = normed.astype(jnp.bfloat16)

    inverse = 1.0 / weight_v[0, 0:1, :]

    def forward(c, rows):
        pre_v[rows, :] = jnp.zeros((rows.size, chunk), jnp.float32)

        @pl.loop(0, blocks)
        def _(k):
            eff_weight = (local_v[c, block_of(k), :].astype(jnp.float32) * inverse).astype(jnp.bfloat16)
            pre_v[rows, :] += jnp.dot(normed_v[rows, block_of(k)], eff_weight, preferred_element_type=jnp.float32)

    def slopes(c, side):
        rows = pl.ds(side * tokens, tokens)
        grad_v[rows, :] = (
            cot_v[side, c].astype(jnp.float32) * silu_slope(scale * pre_v[rows, :])
        ).astype(jnp.bfloat16)

    def backward(c):
        @pl.loop(0, blocks)
        def _(k):
            grad = lax.dot_general(
                normed_v[:, block_of(k)], grad_v[...], (((0,), (0,)), ((), ())), preferred_element_type=jnp.float32
            )
            update = (LEARN_RATE * (scale * grad)).astype(jnp.bfloat16).astype(jnp.float32)
            local_v[c, block_of(k), :] = (local_v[c, block_of(k), :].astype(jnp.float32) - update).astype(jnp.bfloat16)
            send_state(c, k).start()

    own_act.wait()
    normalise(0, 0, tokens)
    load(0).wait()
    forward(0, pl.ds(0, tokens))
    own_cot(0).wait()
    slopes(0, 0)

    @pl.when(jnp.logical_not(leads))
    def _():
        pl.semaphore_wait(go_sem, 1)
        start_sends()

    for i in range(len(pieces)):
        send_act(i).wait_recv()
        normalise(1, *pieces[i])
    forward(0, pl.ds(tokens, tokens))
    send_cot(0).wait_recv()
    slopes(0, 1)
    for c in range(1, chunks):
        send_cot(c).start()

    @pl.when(leads)
    def _():
        pl.semaphore_signal(go_sem, inc=1, device_id=sibling, device_id_type=MESH)

    backward(0)

    @pl.loop(1, chunks)
    def _(c):
        load(c).wait()
        forward(c, pl.ds(0, 2 * tokens))
        own_cot(c).wait()
        slopes(c, 0)
        send_cot(c).wait_recv()
        slopes(c, 1)
        backward(c)

    send_weight.wait_recv()
    new_weight_ref[0] = jnp.max(0.5 * (weight_v[0] + weight_v[1]))

    @pl.loop(0, chunks)
    def _(c):
        @pl.loop(0, blocks)
        def _(k):
            send_state(c, k).wait_recv()
            both = local_v[c, block_of(k), :].astype(jnp.float32) + theirs_v[c, block_of(k), :].astype(jnp.float32)
            theirs_v[c, block_of(k), :] = (0.5 * both).astype(jnp.bfloat16)
            store(c, k).start()

    for i in range(len(pieces)):
        send_act(i).wait_send()
    send_weight.wait_send()

    @pl.loop(0, chunks)
    def _(c):
        send_cot(c).wait_send()

        @pl.loop(0, blocks)
        def _(k):
            send_state(c, k).wait_send()
            store(c, k).wait()


def push(state, hop_size, collective_id):
    numerator, push_weight, norm_gain, activations, cotangent = state
    depth, width = numerator.shape
    tokens = activations.shape[0]
    chunks, blocks = width // CHUNK, depth // BLOCK
    vmem, hbm = pl.BlockSpec(memory_space=pltpu.VMEM), pl.BlockSpec(memory_space=pl.ANY)
    smem = pl.BlockSpec(memory_space=pltpu.SMEM)
    dma = pltpu.SemaphoreType.DMA
    arrivals = -(-tokens // PIECE)
    return pl.pallas_call(
        partial(push_kernel, hop_size),
        out_shape=(
            jax.ShapeDtypeStruct((depth, width), jnp.bfloat16),
            jax.ShapeDtypeStruct((1,), jnp.float32),
        ),
        in_specs=[smem, vmem, hbm, hbm, hbm],
        out_specs=(hbm, smem),
        scratch_shapes=[
            pltpu.VMEM((2, tokens, depth), jnp.bfloat16),
            pltpu.VMEM((2, chunks, tokens, CHUNK), jnp.bfloat16),
            pltpu.VMEM((2 * tokens, depth), jnp.bfloat16),
            pltpu.VMEM((2 * tokens, CHUNK), jnp.float32),
            pltpu.VMEM((2 * tokens, CHUNK), jnp.bfloat16),
            pltpu.VMEM((chunks, depth, CHUNK), jnp.bfloat16),
            pltpu.VMEM((chunks, depth, CHUNK), jnp.bfloat16),
            pltpu.VMEM((2, 8, CHUNK), jnp.float32),
            dma((chunks,)), dma, dma((arrivals,)), dma((arrivals,)), dma((chunks,)), dma((chunks,)), dma((chunks,)),
            dma((chunks, blocks)), dma((chunks, blocks)), dma, dma, dma((chunks, blocks)),
            pltpu.SemaphoreType.REGULAR,
        ],
        compiler_params=pltpu.CompilerParams(
            collective_id=collective_id, has_side_effects=True, vmem_limit_bytes=48 * 2**20
        ),
        cost_estimate=pl.CostEstimate(
            flops=8 * tokens * depth * width, bytes_accessed=4 * depth * width, transcendentals=2 * tokens * width
        ),
    )(push_weight, norm_gain, numerator, activations, cotangent)


def on_pairs(numerator, push_weight, norm_gain, activations, cotangent, step_index):
    depth = numerator.shape[1]
    state = (
        numerator[0], push_weight, norm_gain,
        activations.reshape(-1, depth), cotangent.reshape(-1, cotangent.shape[2]),
    )
    bit_count = lax.axis_size("rep").bit_length() - 1
    branches = [partial(push, hop_size=2**bit, collective_id=bit) for bit in range(bit_count)]
    mixed, new_weight = lax.switch(step_index % bit_count, branches, state)
    return mixed[None], new_weight


def solution(mesh):
    placed = (
        P("rep", None, "fsdp"),
        P("rep"),
        P(),
        P(None, ("rep", "fsdp"), None),
        P(None, ("rep", "fsdp"), None),
        P(),
    )
    return jax.shard_map(
        on_pairs if mesh.shape["fsdp"] == 2 else on_device,
        mesh=mesh,
        in_specs=placed,
        out_specs=(P("rep", None, "fsdp"), P("rep")),
        check_vma=False,
    )
```

```python
from functools import partial

import jax
import jax.numpy as jnp
from jax import lax
from jax.experimental import pallas as pl
from jax.experimental.pallas import tpu as pltpu
from jax.sharding import PartitionSpec as P

LEARN_RATE = 1.5
EPSILON = 1e-05
PIECES = 4
CHUNK = 256
BLOCK = 512
ROWS = 16
PIECE = 48
MESH = pl.DeviceIdType.MESH


def shifted(block, axis, distance):
    count = lax.axis_size(axis)
    route = [((i - distance) % count, i) for i in range(count)]
    return lax.ppermute(block, axis, route)


def silu_slope(pre_act):
    sig = jax.nn.sigmoid(pre_act)
    return sig * (1.0 + pre_act * (1.0 - sig))


def normalised(activations, norm_gain):
    wide = activations.astype(jnp.float32)
    mean_square = jnp.mean(wide * wide, axis=-1, keepdims=True)
    return (wide * lax.rsqrt(mean_square + EPSILON) * norm_gain).astype(jnp.bfloat16)


def token_rows(activations, cotangent):
    count = lax.axis_size("fsdp")
    me = lax.axis_index("fsdp")
    width = cotangent.shape[2] // count
    acts, cots = [activations], [lax.dynamic_slice_in_dim(cotangent, me * width, width, 2)]
    for step in range(1, count):
        acts.append(shifted(activations, "fsdp", step))
        theirs = lax.rem(me + step, count)
        cots.append(shifted(lax.dynamic_slice_in_dim(cotangent, theirs * width, width, 2), "fsdp", step))
    return jnp.concatenate(acts, axis=1), jnp.concatenate(cots, axis=1)


def mix(state, hop_size):
    numerator, push_weight, normed, grad_out = state
    depth = numerator.shape[0]
    scale = depth ** (-0.5)
    rows = depth // PIECES
    mixed = []
    partner_weight = shifted(push_weight, "rep", hop_size)
    for start in range(0, depth, rows):
        grad = scale * jnp.einsum(
            "td,th->dh", normed[:, start : start + rows], grad_out, preferred_element_type=jnp.float32
        )
        update = (LEARN_RATE * grad).astype(jnp.bfloat16).astype(jnp.float32)
        local = (numerator[start : start + rows].astype(jnp.float32) - update).astype(jnp.bfloat16)
        theirs = shifted(local, "rep", hop_size)
        mixed.append((0.5 * (local.astype(jnp.float32) + theirs.astype(jnp.float32))).astype(jnp.bfloat16))
    return jnp.concatenate(mixed, axis=0), 0.5 * (push_weight + partner_weight)


def on_device(numerator, push_weight, norm_gain, activations, cotangent, step_index):
    acts, cots = token_rows(activations, cotangent)
    depth, width = numerator.shape[1:]
    scale = depth ** (-0.5)
    normed = normalised(acts, norm_gain).reshape(-1, depth)
    cots = cots.reshape(-1, width)
    eff_weight = (numerator[0].astype(jnp.float32) / push_weight[0]).astype(jnp.bfloat16)
    pre_act = scale * jnp.dot(normed, eff_weight, preferred_element_type=jnp.float32)
    grad_out = (cots.astype(jnp.float32) * silu_slope(pre_act)).astype(jnp.bfloat16)
    bit_count = lax.axis_size("rep").bit_length() - 1
    branches = [partial(mix, hop_size=2**bit) for bit in range(bit_count)]
    mixed, new_weight = lax.switch(
        step_index % bit_count, branches, (numerator[0], push_weight, normed, grad_out)
    )
    return mixed[None], new_weight


def push_kernel(
    hop_size, weight_ref, gain_ref, numer_hbm, act_hbm, cot_hbm, mixed_hbm, new_weight_ref,
    act_v, cot_v, normed_v, turned_v, pre_v, grad_v, local_v, theirs_v, weight_v,
    load_sem, act_sem, act_send, act_recv, cot_sem, cot_send, cot_recv,
    state_send, state_recv, weight_send, weight_recv, out_sem, go_sem,
):
    rep, col = lax.axis_index("rep"), lax.axis_index("fsdp")
    n_rep = lax.axis_size("rep")
    mate = (rep, 1 - col)
    target = (lax.rem(rep + hop_size, n_rep), col)
    source = (lax.rem(rep + n_rep - hop_size, n_rep), col)
    odd = lax.rem(rep, 2)
    sibling = (rep + 1 - 2 * odd, col)
    leads = odd == (1 if hop_size == 1 else 0)
    tokens, depth = act_hbm.shape
    chunks, _, chunk = local_v.shape
    blocks = depth // BLOCK
    width = chunks * chunk
    scale = depth ** (-0.5)
    pieces = [(first, min(PIECE, tokens - first)) for first in range(0, tokens, PIECE)]

    def columns_of(c):
        return pl.ds(pl.multiple_of(c * chunk, chunk), chunk)

    def block_of(k):
        return pl.ds(pl.multiple_of(k * BLOCK, BLOCK), BLOCK)

    def load(c):
        return pltpu.make_async_copy(numer_hbm.at[:, columns_of(c)], local_v.at[c], load_sem.at[c])

    def own_cot(c):
        columns = pl.ds(pl.multiple_of(col * width + c * chunk, chunk), chunk)
        return pltpu.make_async_copy(cot_hbm.at[:, columns], cot_v.at[0, c], cot_sem.at[c])

    def send_cot(c):
        columns = pl.ds(pl.multiple_of((1 - col) * width + c * chunk, chunk), chunk)
        return pltpu.make_async_remote_copy(
            src_ref=cot_hbm.at[:, columns], dst_ref=cot_v.at[1, c],
            send_sem=cot_send.at[c], recv_sem=cot_recv.at[c], device_id=mate, device_id_type=MESH,
        )

    def send_act(i):
        rows = pl.ds(*pieces[i])
        return pltpu.make_async_remote_copy(
            src_ref=act_hbm.at[rows], dst_ref=act_v.at[1, rows],
            send_sem=act_send.at[i], recv_sem=act_recv.at[i], device_id=mate, device_id_type=MESH,
        )

    def send_state(c, k):
        return pltpu.make_async_remote_copy(
            src_ref=local_v.at[c, block_of(k)], dst_ref=theirs_v.at[c, block_of(k)],
            send_sem=state_send.at[c, k], recv_sem=state_recv.at[c, k], device_id=target, device_id_type=MESH,
        )

    def store(c, k):
        return pltpu.make_async_copy(
            theirs_v.at[c, block_of(k)], mixed_hbm.at[block_of(k), columns_of(c)], out_sem.at[c, k]
        )

    def start_sends():
        for i in range(len(pieces)):
            send_act(i).start()
        send_cot(0).start()

    send_weight = pltpu.make_async_remote_copy(
        src_ref=weight_v.at[0], dst_ref=weight_v.at[1],
        send_sem=weight_send, recv_sem=weight_recv, device_id=target, device_id_type=MESH,
    )
    own_act = pltpu.make_async_copy(act_hbm, act_v.at[0], act_sem)

    barrier = pltpu.get_barrier_semaphore()
    for device in (mate, source, sibling):
        pl.semaphore_signal(barrier, inc=1, device_id=device, device_id_type=MESH)
    own_act.start()
    weight_v[0] = jnp.full(weight_v.shape[1:], weight_ref[0], jnp.float32)
    pl.semaphore_wait(barrier, 3)

    @pl.when(leads)
    def _():
        start_sends()

    send_weight.start()
    for c in range(chunks):
        own_cot(c).start()
        load(c).start()

    gain = gain_ref[...].reshape(1, depth)

    def normalise(side, first, count):
        @pl.loop(0, count // ROWS)
        def _(i):
            rows = pl.ds(pl.multiple_of(first + i * ROWS, ROWS), ROWS)
            wide = act_v[side, rows, :].astype(jnp.float32)
            mean_square = jnp.mean(wide * wide, axis=-1, keepdims=True)
            normed = wide * lax.rsqrt(mean_square + EPSILON) * gain
            normed_v[pl.ds(pl.multiple_of(side * tokens + first + i * ROWS, ROWS), ROWS), :] = normed.astype(jnp.bfloat16)

    inverse = 1.0 / weight_v[0, 0:1, :]

    def forward(c, rows):
        pre_v[rows, :] = jnp.zeros((rows.size, chunk), jnp.float32)

        @pl.loop(0, blocks, unroll=True)
        def _(k):
            eff_weight = (local_v[c, block_of(k), :].astype(jnp.float32) * inverse).astype(jnp.bfloat16)
            pre_v[rows, :] += jnp.dot(normed_v[rows, block_of(k)], eff_weight, preferred_element_type=jnp.float32)

    def slopes(c, side):
        rows = pl.ds(side * tokens, tokens)
        grad_v[rows, :] = (
            cot_v[side, c].astype(jnp.float32) * silu_slope(scale * pre_v[rows, :])
        ).astype(jnp.bfloat16)

    def turn(side, k):
        turned_v[side, block_of(k), :] = normed_v[pl.ds(side * tokens, tokens), block_of(k)].T

    def backward(c, first=False):
        @pl.loop(0, blocks, unroll=True)
        def _(k):
            if first:
                turn(1, k)
            grad = sum(
                jnp.dot(
                    turned_v[side, block_of(k), :], grad_v[pl.ds(side * tokens, tokens), :],
                    preferred_element_type=jnp.float32,
                )
                for side in range(2)
            )
            update = (LEARN_RATE * (scale * grad)).astype(jnp.bfloat16).astype(jnp.float32)
            local_v[c, block_of(k), :] = (local_v[c, block_of(k), :].astype(jnp.float32) - update).astype(jnp.bfloat16)
            send_state(c, k).start()

    own_act.wait()
    normalise(0, 0, tokens)
    load(0).wait()
    forward(0, pl.ds(0, tokens))
    own_cot(0).wait()
    slopes(0, 0)

    @pl.loop(0, blocks)
    def _(k):
        turn(0, k)

    @pl.when(jnp.logical_not(leads))
    def _():
        pl.semaphore_wait(go_sem, 1)
        start_sends()

    for i in range(len(pieces)):
        send_act(i).wait_recv()
        normalise(1, *pieces[i])
        if i == len(pieces) - 2:

            @pl.when(leads)
            def _():
                pl.semaphore_signal(go_sem, inc=1, device_id=sibling, device_id_type=MESH)

    forward(0, pl.ds(tokens, tokens))
    send_cot(0).wait_recv()
    slopes(0, 1)
    for c in range(1, chunks):
        send_cot(c).start()

    backward(0, first=True)

    @pl.loop(1, chunks)
    def _(c):
        load(c).wait()
        forward(c, pl.ds(0, 2 * tokens))
        own_cot(c).wait()
        slopes(c, 0)
        send_cot(c).wait_recv()
        slopes(c, 1)
        backward(c)

    send_weight.wait_recv()
    new_weight_ref[0] = jnp.max(0.5 * (weight_v[0] + weight_v[1]))

    @pl.loop(0, chunks)
    def _(c):
        @pl.loop(0, blocks)
        def _(k):
            send_state(c, k).wait_recv()
            both = local_v[c, block_of(k), :].astype(jnp.float32) + theirs_v[c, block_of(k), :].astype(jnp.float32)
            theirs_v[c, block_of(k), :] = (0.5 * both).astype(jnp.bfloat16)
            store(c, k).start()

    for i in range(len(pieces)):
        send_act(i).wait_send()
    send_weight.wait_send()

    @pl.loop(0, chunks)
    def _(c):
        send_cot(c).wait_send()

        @pl.loop(0, blocks)
        def _(k):
            send_state(c, k).wait_send()
            store(c, k).wait()


def push(state, hop_size, collective_id):
    numerator, push_weight, norm_gain, activations, cotangent = state
    depth, width = numerator.shape
    tokens = activations.shape[0]
    chunks, blocks = width // CHUNK, depth // BLOCK
    vmem, hbm = pl.BlockSpec(memory_space=pltpu.VMEM), pl.BlockSpec(memory_space=pl.ANY)
    smem = pl.BlockSpec(memory_space=pltpu.SMEM)
    dma = pltpu.SemaphoreType.DMA
    arrivals = -(-tokens // PIECE)
    return pl.pallas_call(
        partial(push_kernel, hop_size),
        out_shape=(
            jax.ShapeDtypeStruct((depth, width), jnp.bfloat16),
            jax.ShapeDtypeStruct((1,), jnp.float32),
        ),
        in_specs=[smem, vmem, hbm, hbm, hbm],
        out_specs=(hbm, smem),
        scratch_shapes=[
            pltpu.VMEM((2, tokens, depth), jnp.bfloat16),
            pltpu.VMEM((2, chunks, tokens, CHUNK), jnp.bfloat16),
            pltpu.VMEM((2 * tokens, depth), jnp.bfloat16),
            pltpu.VMEM((2, depth, tokens), jnp.bfloat16),
            pltpu.VMEM((2 * tokens, CHUNK), jnp.float32),
            pltpu.VMEM((2 * tokens, CHUNK), jnp.bfloat16),
            pltpu.VMEM((chunks, depth, CHUNK), jnp.bfloat16),
            pltpu.VMEM((chunks, depth, CHUNK), jnp.bfloat16),
            pltpu.VMEM((2, 8, CHUNK), jnp.float32),
            dma((chunks,)), dma, dma((arrivals,)), dma((arrivals,)), dma((chunks,)), dma((chunks,)), dma((chunks,)),
            dma((chunks, blocks)), dma((chunks, blocks)), dma, dma, dma((chunks, blocks)),
            pltpu.SemaphoreType.REGULAR,
        ],
        compiler_params=pltpu.CompilerParams(
            collective_id=collective_id, has_side_effects=True, vmem_limit_bytes=48 * 2**20
        ),
        cost_estimate=pl.CostEstimate(
            flops=8 * tokens * depth * width, bytes_accessed=4 * depth * width, transcendentals=2 * tokens * width
        ),
    )(push_weight, norm_gain, numerator, activations, cotangent)


def on_pairs(numerator, push_weight, norm_gain, activations, cotangent, step_index):
    depth = numerator.shape[1]
    state = (
        numerator[0], push_weight, norm_gain,
        activations.reshape(-1, depth), cotangent.reshape(-1, cotangent.shape[2]),
    )
    bit_count = lax.axis_size("rep").bit_length() - 1
    branches = [partial(push, hop_size=2**bit, collective_id=bit) for bit in range(bit_count)]
    mixed, new_weight = lax.switch(step_index % bit_count, branches, state)
    return mixed[None], new_weight


def solution(mesh):
    placed = (
        P("rep", None, "fsdp"),
        P("rep"),
        P(),
        P(None, ("rep", "fsdp"), None),
        P(None, ("rep", "fsdp"), None),
        P(),
    )
    return jax.shard_map(
        on_pairs if mesh.shape["fsdp"] == 2 else on_device,
        mesh=mesh,
        in_specs=placed,
        out_specs=(P("rep", None, "fsdp"), P("rep")),
        check_vma=False,
    )
```

```python
from functools import partial

import jax
import jax.numpy as jnp
from jax import lax
from jax.experimental import pallas as pl
from jax.experimental.pallas import tpu as pltpu
from jax.sharding import PartitionSpec as P

LEARN_RATE = 1.5
EPSILON = 1e-05
PIECES = 4
CHUNK = 256
BLOCK = 512
ROWS = 16
PIECE = 48
MESH = pl.DeviceIdType.MESH


def shifted(block, axis, distance):
    count = lax.axis_size(axis)
    route = [((i - distance) % count, i) for i in range(count)]
    return lax.ppermute(block, axis, route)


def silu_slope(pre_act):
    sig = jax.nn.sigmoid(pre_act)
    return sig * (1.0 + pre_act * (1.0 - sig))


def normalised(activations, norm_gain):
    wide = activations.astype(jnp.float32)
    mean_square = jnp.mean(wide * wide, axis=-1, keepdims=True)
    return (wide * lax.rsqrt(mean_square + EPSILON) * norm_gain).astype(jnp.bfloat16)


def token_rows(activations, cotangent):
    count = lax.axis_size("fsdp")
    me = lax.axis_index("fsdp")
    width = cotangent.shape[2] // count
    acts, cots = [activations], [lax.dynamic_slice_in_dim(cotangent, me * width, width, 2)]
    for step in range(1, count):
        acts.append(shifted(activations, "fsdp", step))
        theirs = lax.rem(me + step, count)
        cots.append(shifted(lax.dynamic_slice_in_dim(cotangent, theirs * width, width, 2), "fsdp", step))
    return jnp.concatenate(acts, axis=1), jnp.concatenate(cots, axis=1)


def mix(state, hop_size):
    numerator, push_weight, normed, grad_out = state
    depth = numerator.shape[0]
    scale = depth ** (-0.5)
    rows = depth // PIECES
    mixed = []
    partner_weight = shifted(push_weight, "rep", hop_size)
    for start in range(0, depth, rows):
        grad = scale * jnp.einsum(
            "td,th->dh", normed[:, start : start + rows], grad_out, preferred_element_type=jnp.float32
        )
        update = (LEARN_RATE * grad).astype(jnp.bfloat16).astype(jnp.float32)
        local = (numerator[start : start + rows].astype(jnp.float32) - update).astype(jnp.bfloat16)
        theirs = shifted(local, "rep", hop_size)
        mixed.append((0.5 * (local.astype(jnp.float32) + theirs.astype(jnp.float32))).astype(jnp.bfloat16))
    return jnp.concatenate(mixed, axis=0), 0.5 * (push_weight + partner_weight)


def on_device(numerator, push_weight, norm_gain, activations, cotangent, step_index):
    acts, cots = token_rows(activations, cotangent)
    depth, width = numerator.shape[1:]
    scale = depth ** (-0.5)
    normed = normalised(acts, norm_gain).reshape(-1, depth)
    cots = cots.reshape(-1, width)
    eff_weight = (numerator[0].astype(jnp.float32) / push_weight[0]).astype(jnp.bfloat16)
    pre_act = scale * jnp.dot(normed, eff_weight, preferred_element_type=jnp.float32)
    grad_out = (cots.astype(jnp.float32) * silu_slope(pre_act)).astype(jnp.bfloat16)
    bit_count = lax.axis_size("rep").bit_length() - 1
    branches = [partial(mix, hop_size=2**bit) for bit in range(bit_count)]
    mixed, new_weight = lax.switch(
        step_index % bit_count, branches, (numerator[0], push_weight, normed, grad_out)
    )
    return mixed[None], new_weight


def push_kernel(
    hop_size, weight_ref, gain_ref, numer_hbm, act_hbm, cot_hbm, mixed_hbm, new_weight_ref,
    act_v, cot_v, normed_v, turned_v, pre_v, grad_v, local_v, theirs_v, weight_v,
    load_sem, act_sem, act_send, act_recv, cot_sem, cot_send, cot_recv,
    state_send, state_recv, weight_send, weight_recv, out_sem, go_sem,
):
    rep, col = lax.axis_index("rep"), lax.axis_index("fsdp")
    n_rep = lax.axis_size("rep")
    mate = (rep, 1 - col)
    target = (lax.rem(rep + hop_size, n_rep), col)
    source = (lax.rem(rep + n_rep - hop_size, n_rep), col)
    odd = lax.rem(rep, 2)
    sibling = (rep + 1 - 2 * odd, col)
    leads = odd == (1 if hop_size == 1 else 0)
    tokens, depth = act_hbm.shape
    chunks, _, chunk = local_v.shape
    blocks = depth // BLOCK
    width = chunks * chunk
    scale = depth ** (-0.5)
    pieces = [(first, min(PIECE, tokens - first)) for first in range(0, tokens, PIECE)]

    def columns_of(c):
        return pl.ds(pl.multiple_of(c * chunk, chunk), chunk)

    def block_of(k):
        return pl.ds(pl.multiple_of(k * BLOCK, BLOCK), BLOCK)

    def load(c):
        return pltpu.make_async_copy(numer_hbm.at[:, columns_of(c)], local_v.at[c], load_sem.at[c])

    def own_cot(c):
        columns = pl.ds(pl.multiple_of(col * width + c * chunk, chunk), chunk)
        return pltpu.make_async_copy(cot_hbm.at[:, columns], cot_v.at[0, c], cot_sem.at[c])

    def send_cot(c):
        columns = pl.ds(pl.multiple_of((1 - col) * width + c * chunk, chunk), chunk)
        return pltpu.make_async_remote_copy(
            src_ref=cot_hbm.at[:, columns], dst_ref=cot_v.at[1, c],
            send_sem=cot_send.at[c], recv_sem=cot_recv.at[c], device_id=mate, device_id_type=MESH,
        )

    def send_act(i):
        rows = pl.ds(*pieces[i])
        return pltpu.make_async_remote_copy(
            src_ref=act_hbm.at[rows], dst_ref=act_v.at[1, rows],
            send_sem=act_send.at[i], recv_sem=act_recv.at[i], device_id=mate, device_id_type=MESH,
        )

    def send_state(c, k):
        return pltpu.make_async_remote_copy(
            src_ref=local_v.at[c, block_of(k)], dst_ref=theirs_v.at[c, block_of(k)],
            send_sem=state_send.at[c, k], recv_sem=state_recv.at[c, k], device_id=target, device_id_type=MESH,
        )

    def store(c, k):
        return pltpu.make_async_copy(
            theirs_v.at[c, block_of(k)], mixed_hbm.at[block_of(k), columns_of(c)], out_sem.at[c, k]
        )

    def start_sends():
        for i in range(len(pieces)):
            send_act(i).start()
        send_cot(0).start()

    send_weight = pltpu.make_async_remote_copy(
        src_ref=weight_v.at[0], dst_ref=weight_v.at[1],
        send_sem=weight_send, recv_sem=weight_recv, device_id=target, device_id_type=MESH,
    )
    own_act = pltpu.make_async_copy(act_hbm, act_v.at[0], act_sem)

    barrier = pltpu.get_barrier_semaphore()
    for device in (mate, source, sibling):
        pl.semaphore_signal(barrier, inc=1, device_id=device, device_id_type=MESH)
    own_act.start()
    load(0).start()
    own_cot(0).start()
    weight_v[0] = jnp.full(weight_v.shape[1:], weight_ref[0], jnp.float32)
    pl.semaphore_wait(barrier, 3)

    @pl.when(leads)
    def _():
        start_sends()

    send_weight.start()

    gain = gain_ref[...].reshape(1, depth)

    def normalise(side, first, count):
        @pl.loop(0, count // ROWS)
        def _(i):
            rows = pl.ds(pl.multiple_of(first + i * ROWS, ROWS), ROWS)
            wide = act_v[side, rows, :].astype(jnp.float32)
            mean_square = jnp.mean(wide * wide, axis=-1, keepdims=True)
            normed = wide * lax.rsqrt(mean_square + EPSILON) * gain
            normed_v[pl.ds(pl.multiple_of(side * tokens + first + i * ROWS, ROWS), ROWS), :] = normed.astype(jnp.bfloat16)

    inverse = 1.0 / weight_v[0, 0:1, :]

    def forward(c, rows):
        pre_v[rows, :] = jnp.zeros((rows.size, chunk), jnp.float32)

        @pl.loop(0, blocks, unroll=True)
        def _(k):
            eff_weight = (local_v[c, block_of(k), :].astype(jnp.float32) * inverse).astype(jnp.bfloat16)
            pre_v[rows, :] += jnp.dot(normed_v[rows, block_of(k)], eff_weight, preferred_element_type=jnp.float32)

    def slopes(c, side):
        rows = pl.ds(side * tokens, tokens)
        grad_v[rows, :] = (
            cot_v[side, c].astype(jnp.float32) * silu_slope(scale * pre_v[rows, :])
        ).astype(jnp.bfloat16)

    def turn(side, k):
        turned_v[side, block_of(k), :] = normed_v[pl.ds(side * tokens, tokens), block_of(k)].T

    def backward(c, first=False):
        @pl.loop(0, blocks, unroll=True)
        def _(k):
            if first:
                turn(1, k)
            grad = sum(
                jnp.dot(
                    turned_v[side, block_of(k), :], grad_v[pl.ds(side * tokens, tokens), :],
                    preferred_element_type=jnp.float32,
                )
                for side in range(2)
            )
            update = (LEARN_RATE * (scale * grad)).astype(jnp.bfloat16).astype(jnp.float32)
            local_v[c, block_of(k), :] = (local_v[c, block_of(k), :].astype(jnp.float32) - update).astype(jnp.bfloat16)
            send_state(c, k).start()

    own_act.wait()
    normalise(0, 0, tokens)
    load(0).wait()
    forward(0, pl.ds(0, tokens))
    own_cot(0).wait()
    slopes(0, 0)

    @pl.loop(0, blocks)
    def _(k):
        turn(0, k)

    @pl.when(jnp.logical_not(leads))
    def _():
        pl.semaphore_wait(go_sem, 1)
        start_sends()

    for i in range(len(pieces)):
        send_act(i).wait_recv()
        normalise(1, *pieces[i])
        if i == 0:
            for c in range(1, chunks):
                own_cot(c).start()
                load(c).start()
        if i == 1:

            @pl.when(leads)
            def _():
                pl.semaphore_signal(go_sem, inc=1, device_id=sibling, device_id_type=MESH)

    forward(0, pl.ds(tokens, tokens))
    send_cot(0).wait_recv()
    slopes(0, 1)
    for c in range(1, chunks):
        send_cot(c).start()

    backward(0, first=True)

    @pl.loop(1, chunks)
    def _(c):
        load(c).wait()
        forward(c, pl.ds(0, 2 * tokens))
        own_cot(c).wait()
        slopes(c, 0)
        send_cot(c).wait_recv()
        slopes(c, 1)
        backward(c)

    send_weight.wait_recv()
    new_weight_ref[0] = jnp.max(0.5 * (weight_v[0] + weight_v[1]))

    @pl.loop(0, chunks)
    def _(c):
        @pl.loop(0, blocks)
        def _(k):
            send_state(c, k).wait_recv()
            both = local_v[c, block_of(k), :].astype(jnp.float32) + theirs_v[c, block_of(k), :].astype(jnp.float32)
            theirs_v[c, block_of(k), :] = (0.5 * both).astype(jnp.bfloat16)
            store(c, k).start()

    for i in range(len(pieces)):
        send_act(i).wait_send()
    send_weight.wait_send()

    @pl.loop(0, chunks)
    def _(c):
        send_cot(c).wait_send()

        @pl.loop(0, blocks)
        def _(k):
            send_state(c, k).wait_send()
            store(c, k).wait()


def push(state, hop_size, collective_id):
    numerator, push_weight, norm_gain, activations, cotangent = state
    depth, width = numerator.shape
    tokens = activations.shape[0]
    chunks, blocks = width // CHUNK, depth // BLOCK
    vmem, hbm = pl.BlockSpec(memory_space=pltpu.VMEM), pl.BlockSpec(memory_space=pl.ANY)
    smem = pl.BlockSpec(memory_space=pltpu.SMEM)
    dma = pltpu.SemaphoreType.DMA
    arrivals = -(-tokens // PIECE)
    return pl.pallas_call(
        partial(push_kernel, hop_size),
        out_shape=(
            jax.ShapeDtypeStruct((depth, width), jnp.bfloat16),
            jax.ShapeDtypeStruct((1,), jnp.float32),
        ),
        in_specs=[smem, vmem, hbm, hbm, hbm],
        out_specs=(hbm, smem),
        scratch_shapes=[
            pltpu.VMEM((2, tokens, depth), jnp.bfloat16),
            pltpu.VMEM((2, chunks, tokens, CHUNK), jnp.bfloat16),
            pltpu.VMEM((2 * tokens, depth), jnp.bfloat16),
            pltpu.VMEM((2, depth, tokens), jnp.bfloat16),
            pltpu.VMEM((2 * tokens, CHUNK), jnp.float32),
            pltpu.VMEM((2 * tokens, CHUNK), jnp.bfloat16),
            pltpu.VMEM((chunks, depth, CHUNK), jnp.bfloat16),
            pltpu.VMEM((chunks, depth, CHUNK), jnp.bfloat16),
            pltpu.VMEM((2, 8, CHUNK), jnp.float32),
            dma((chunks,)), dma, dma((arrivals,)), dma((arrivals,)), dma((chunks,)), dma((chunks,)), dma((chunks,)),
            dma((chunks, blocks)), dma((chunks, blocks)), dma, dma, dma((chunks, blocks)),
            pltpu.SemaphoreType.REGULAR,
        ],
        compiler_params=pltpu.CompilerParams(
            collective_id=collective_id, has_side_effects=True, vmem_limit_bytes=48 * 2**20
        ),
        cost_estimate=pl.CostEstimate(
            flops=8 * tokens * depth * width, bytes_accessed=4 * depth * width, transcendentals=2 * tokens * width
        ),
    )(push_weight, norm_gain, numerator, activations, cotangent)


def on_pairs(numerator, push_weight, norm_gain, activations, cotangent, step_index):
    depth = numerator.shape[1]
    state = (
        numerator[0], push_weight, norm_gain,
        activations.reshape(-1, depth), cotangent.reshape(-1, cotangent.shape[2]),
    )
    bit_count = lax.axis_size("rep").bit_length() - 1
    branches = [partial(push, hop_size=2**bit, collective_id=bit) for bit in range(bit_count)]
    mixed, new_weight = lax.switch(step_index % bit_count, branches, state)
    return mixed[None], new_weight


def solution(mesh):
    placed = (
        P("rep", None, "fsdp"),
        P("rep"),
        P(),
        P(None, ("rep", "fsdp"), None),
        P(None, ("rep", "fsdp"), None),
        P(),
    )
    return jax.shard_map(
        on_pairs if mesh.shape["fsdp"] == 2 else on_device,
        mesh=mesh,
        in_specs=placed,
        out_specs=(P("rep", None, "fsdp"), P("rep")),
        check_vma=False,
    )
```

```python
from functools import partial

import jax
import jax.numpy as jnp
from jax import lax
from jax.experimental import pallas as pl
from jax.experimental.pallas import tpu as pltpu
from jax.sharding import PartitionSpec as P

LEARN_RATE = 1.5
EPSILON = 1e-05
PIECES = 4
CHUNK = 256
BLOCK = 512
ROWS = 16
LANES = 128
SHARES = (64, 64, 32)
MESH = pl.DeviceIdType.MESH


def shifted(block, axis, distance):
    count = lax.axis_size(axis)
    route = [((i - distance) % count, i) for i in range(count)]
    return lax.ppermute(block, axis, route)


def silu_slope(pre_act):
    sig = jax.nn.sigmoid(pre_act)
    return sig * (1.0 + pre_act * (1.0 - sig))


def normalised(activations, norm_gain):
    wide = activations.astype(jnp.float32)
    mean_square = jnp.mean(wide * wide, axis=-1, keepdims=True)
    return (wide * lax.rsqrt(mean_square + EPSILON) * norm_gain).astype(jnp.bfloat16)


def token_rows(activations, cotangent):
    count = lax.axis_size("fsdp")
    me = lax.axis_index("fsdp")
    width = cotangent.shape[2] // count
    acts, cots = [activations], [lax.dynamic_slice_in_dim(cotangent, me * width, width, 2)]
    for step in range(1, count):
        acts.append(shifted(activations, "fsdp", step))
        theirs = lax.rem(me + step, count)
        cots.append(shifted(lax.dynamic_slice_in_dim(cotangent, theirs * width, width, 2), "fsdp", step))
    return jnp.concatenate(acts, axis=1), jnp.concatenate(cots, axis=1)


def mix(state, hop_size):
    numerator, push_weight, normed, grad_out = state
    depth = numerator.shape[0]
    scale = depth ** (-0.5)
    rows = depth // PIECES
    mixed = []
    partner_weight = shifted(push_weight, "rep", hop_size)
    for start in range(0, depth, rows):
        grad = scale * jnp.einsum(
            "td,th->dh", normed[:, start : start + rows], grad_out, preferred_element_type=jnp.float32
        )
        update = (LEARN_RATE * grad).astype(jnp.bfloat16).astype(jnp.float32)
        local = (numerator[start : start + rows].astype(jnp.float32) - update).astype(jnp.bfloat16)
        theirs = shifted(local, "rep", hop_size)
        mixed.append((0.5 * (local.astype(jnp.float32) + theirs.astype(jnp.float32))).astype(jnp.bfloat16))
    return jnp.concatenate(mixed, axis=0), 0.5 * (push_weight + partner_weight)


def on_device(numerator, push_weight, norm_gain, activations, cotangent, step_index):
    acts, cots = token_rows(activations, cotangent)
    depth, width = numerator.shape[1:]
    scale = depth ** (-0.5)
    normed = normalised(acts, norm_gain).reshape(-1, depth)
    cots = cots.reshape(-1, width)
    eff_weight = (numerator[0].astype(jnp.float32) / push_weight[0]).astype(jnp.bfloat16)
    pre_act = scale * jnp.dot(normed, eff_weight, preferred_element_type=jnp.float32)
    grad_out = (cots.astype(jnp.float32) * silu_slope(pre_act)).astype(jnp.bfloat16)
    bit_count = lax.axis_size("rep").bit_length() - 1
    branches = [partial(mix, hop_size=2**bit) for bit in range(bit_count)]
    mixed, new_weight = lax.switch(
        step_index % bit_count, branches, (numerator[0], push_weight, normed, grad_out)
    )
    return mixed[None], new_weight


def pieces_of(tokens):
    pieces, first = [], 0
    for count in SHARES:
        if first + count < tokens:
            pieces.append((first, count))
            first += count
    return pieces + [(first, tokens - first)]


def push_kernel(
    hop_size, weight_ref, gain_ref, numer_hbm, act_hbm, cot_hbm, mixed_hbm, new_weight_ref,
    act_v, cot_v, normed_v, turned_v, pre_v, grad_v, local_v, theirs_v, weight_v, eff_v,
    load_sem, act_sem, act_send, act_recv, cot_sem, cot_send, cot_recv,
    state_send, state_recv, weight_send, weight_recv, out_sem, go_sem,
):
    rep, col = lax.axis_index("rep"), lax.axis_index("fsdp")
    n_rep = lax.axis_size("rep")
    mate = (rep, 1 - col)
    target = (lax.rem(rep + hop_size, n_rep), col)
    source = (lax.rem(rep + n_rep - hop_size, n_rep), col)
    odd = lax.rem(rep, 2)
    sibling = (rep + 1 - 2 * odd, col)
    leads = odd == (1 if hop_size == 1 else 0)
    tokens, depth = act_hbm.shape
    chunks, _, chunk = local_v.shape
    blocks = depth // BLOCK
    width = chunks * chunk
    scale = depth ** (-0.5)
    pieces = pieces_of(tokens)
    early = LANES if any(sum(piece) == LANES for piece in pieces[:-1]) else 0

    def columns_of(c):
        return pl.ds(pl.multiple_of(c * chunk, chunk), chunk)

    def block_of(k):
        return pl.ds(pl.multiple_of(k * BLOCK, BLOCK), BLOCK)

    def load(c):
        return pltpu.make_async_copy(numer_hbm.at[:, columns_of(c)], local_v.at[c], load_sem.at[c])

    def own_cot(c):
        columns = pl.ds(pl.multiple_of(col * width + c * chunk, chunk), chunk)
        return pltpu.make_async_copy(cot_hbm.at[:, columns], cot_v.at[0, c], cot_sem.at[c])

    def send_cot(c):
        columns = pl.ds(pl.multiple_of((1 - col) * width + c * chunk, chunk), chunk)
        return pltpu.make_async_remote_copy(
            src_ref=cot_hbm.at[:, columns], dst_ref=cot_v.at[1, c],
            send_sem=cot_send.at[c], recv_sem=cot_recv.at[c], device_id=mate, device_id_type=MESH,
        )

    def send_act(i):
        rows = pl.ds(*pieces[i])
        return pltpu.make_async_remote_copy(
            src_ref=act_hbm.at[rows], dst_ref=act_v.at[1, rows],
            send_sem=act_send.at[i], recv_sem=act_recv.at[i], device_id=mate, device_id_type=MESH,
        )

    def send_state(c, k):
        return pltpu.make_async_remote_copy(
            src_ref=local_v.at[c, block_of(k)], dst_ref=theirs_v.at[c, block_of(k)],
            send_sem=state_send.at[c, k], recv_sem=state_recv.at[c, k], device_id=target, device_id_type=MESH,
        )

    def store(c, k):
        return pltpu.make_async_copy(
            theirs_v.at[c, block_of(k)], mixed_hbm.at[block_of(k), columns_of(c)], out_sem.at[c, k]
        )

    def start_sends():
        for i in range(len(pieces)):
            send_act(i).start()
        send_cot(0).start()

    send_weight = pltpu.make_async_remote_copy(
        src_ref=weight_v.at[0], dst_ref=weight_v.at[1],
        send_sem=weight_send, recv_sem=weight_recv, device_id=target, device_id_type=MESH,
    )
    own_act = pltpu.make_async_copy(act_hbm, act_v.at[0], act_sem)

    barrier = pltpu.get_barrier_semaphore()
    for device in (mate, source, sibling):
        pl.semaphore_signal(barrier, inc=1, device_id=device, device_id_type=MESH)
    own_act.start()
    load(0).start()
    own_cot(0).start()
    weight_v[0] = jnp.full(weight_v.shape[1:], weight_ref[0], jnp.float32)
    pl.semaphore_wait(barrier, 3)

    @pl.when(leads)
    def _():
        start_sends()

    send_weight.start()
    for c in range(1, chunks):
        own_cot(c).start()
        load(c).start()

    gain = gain_ref[...].reshape(1, depth)

    def normalise(side, first, count):
        @pl.loop(0, count // ROWS)
        def _(i):
            rows = pl.ds(pl.multiple_of(first + i * ROWS, ROWS), ROWS)
            wide = act_v[side, rows, :].astype(jnp.float32)
            mean_square = jnp.mean(wide * wide, axis=-1, keepdims=True)
            normed = wide * lax.rsqrt(mean_square + EPSILON) * gain
            normed_v[pl.ds(pl.multiple_of(side * tokens + first + i * ROWS, ROWS), ROWS), :] = normed.astype(jnp.bfloat16)

    inverse = 1.0 / weight_v[0, 0:1, :]

    def weigh(c):
        @pl.loop(0, blocks)
        def _(k):
            eff_v[block_of(k), :] = (local_v[c, block_of(k), :].astype(jnp.float32) * inverse).astype(jnp.bfloat16)

    def forward(first, count):
        rows = pl.ds(first, count)
        pre_v[rows, :] = jnp.dot(normed_v[rows, :], eff_v[...], preferred_element_type=jnp.float32)

    def slopes(c, side):
        rows = pl.ds(side * tokens, tokens)
        grad_v[rows, :] = (
            cot_v[side, c].astype(jnp.float32) * silu_slope(scale * pre_v[rows, :])
        ).astype(jnp.bfloat16)

    def turn(side, k, first, count):
        turned_v[side, block_of(k), pl.ds(first, count)] = normed_v[pl.ds(side * tokens + first, count), block_of(k)].T

    def backward(c, first=False):
        @pl.loop(0, blocks, unroll=True)
        def _(k):
            if first:
                turn(1, k, early, tokens - early)
            grad = sum(
                jnp.dot(
                    turned_v[side, block_of(k), :], grad_v[pl.ds(side * tokens, tokens), :],
                    preferred_element_type=jnp.float32,
                )
                for side in range(2)
            )
            update = (LEARN_RATE * (scale * grad)).astype(jnp.bfloat16).astype(jnp.float32)
            local_v[c, block_of(k), :] = (local_v[c, block_of(k), :].astype(jnp.float32) - update).astype(jnp.bfloat16)
            send_state(c, k).start()

    own_act.wait()
    normalise(0, 0, tokens)
    load(0).wait()
    weigh(0)
    forward(0, tokens)
    own_cot(0).wait()
    slopes(0, 0)

    @pl.loop(0, blocks)
    def _(k):
        turn(0, k, 0, tokens)

    @pl.when(jnp.logical_not(leads))
    def _():
        pl.semaphore_wait(go_sem, 1)
        start_sends()

    for i in range(len(pieces)):
        send_act(i).wait_recv()
        normalise(1, *pieces[i])
        forward(tokens + pieces[i][0], pieces[i][1])
        if sum(pieces[i]) == early:

            @pl.loop(0, blocks)
            def _(k):
                turn(1, k, 0, early)

    send_cot(0).wait_recv()
    for c in range(1, chunks):
        send_cot(c).start()

    @pl.when(leads)
    def _():
        pl.semaphore_signal(go_sem, inc=1, device_id=sibling, device_id_type=MESH)

    slopes(0, 1)

    backward(0, first=True)

    @pl.loop(1, chunks)
    def _(c):
        load(c).wait()
        weigh(c)
        forward(0, 2 * tokens)
        own_cot(c).wait()
        slopes(c, 0)
        send_cot(c).wait_recv()
        slopes(c, 1)
        backward(c)

    send_weight.wait_recv()
    new_weight_ref[0] = jnp.max(0.5 * (weight_v[0] + weight_v[1]))

    @pl.loop(0, chunks)
    def _(c):
        @pl.loop(0, blocks)
        def _(k):
            send_state(c, k).wait_recv()
            both = local_v[c, block_of(k), :].astype(jnp.float32) + theirs_v[c, block_of(k), :].astype(jnp.float32)
            theirs_v[c, block_of(k), :] = (0.5 * both).astype(jnp.bfloat16)
            store(c, k).start()

    for i in range(len(pieces)):
        send_act(i).wait_send()
    send_weight.wait_send()

    @pl.loop(0, chunks)
    def _(c):
        send_cot(c).wait_send()

        @pl.loop(0, blocks)
        def _(k):
            send_state(c, k).wait_send()
            store(c, k).wait()


def push(state, hop_size, collective_id):
    numerator, push_weight, norm_gain, activations, cotangent = state
    depth, width = numerator.shape
    tokens = activations.shape[0]
    chunks, blocks = width // CHUNK, depth // BLOCK
    vmem, hbm = pl.BlockSpec(memory_space=pltpu.VMEM), pl.BlockSpec(memory_space=pl.ANY)
    smem = pl.BlockSpec(memory_space=pltpu.SMEM)
    dma = pltpu.SemaphoreType.DMA
    arrivals = len(pieces_of(tokens))
    return pl.pallas_call(
        partial(push_kernel, hop_size),
        out_shape=(
            jax.ShapeDtypeStruct((depth, width), jnp.bfloat16),
            jax.ShapeDtypeStruct((1,), jnp.float32),
        ),
        in_specs=[smem, vmem, hbm, hbm, hbm],
        out_specs=(hbm, smem),
        scratch_shapes=[
            pltpu.VMEM((2, tokens, depth), jnp.bfloat16),
            pltpu.VMEM((2, chunks, tokens, CHUNK), jnp.bfloat16),
            pltpu.VMEM((2 * tokens, depth), jnp.bfloat16),
            pltpu.VMEM((2, depth, tokens), jnp.bfloat16),
            pltpu.VMEM((2 * tokens, CHUNK), jnp.float32),
            pltpu.VMEM((2 * tokens, CHUNK), jnp.bfloat16),
            pltpu.VMEM((chunks, depth, CHUNK), jnp.bfloat16),
            pltpu.VMEM((chunks, depth, CHUNK), jnp.bfloat16),
            pltpu.VMEM((2, 8, CHUNK), jnp.float32),
            pltpu.VMEM((depth, CHUNK), jnp.bfloat16),
            dma((chunks,)), dma, dma((arrivals,)), dma((arrivals,)), dma((chunks,)), dma((chunks,)), dma((chunks,)),
            dma((chunks, blocks)), dma((chunks, blocks)), dma, dma, dma((chunks, blocks)),
            pltpu.SemaphoreType.REGULAR,
        ],
        compiler_params=pltpu.CompilerParams(
            collective_id=collective_id, has_side_effects=True, vmem_limit_bytes=48 * 2**20
        ),
        cost_estimate=pl.CostEstimate(
            flops=8 * tokens * depth * width, bytes_accessed=4 * depth * width, transcendentals=2 * tokens * width
        ),
    )(push_weight, norm_gain, numerator, activations, cotangent)


def on_pairs(numerator, push_weight, norm_gain, activations, cotangent, step_index):
    depth = numerator.shape[1]
    state = (
        numerator[0], push_weight, norm_gain,
        activations.reshape(-1, depth), cotangent.reshape(-1, cotangent.shape[2]),
    )
    bit_count = lax.axis_size("rep").bit_length() - 1
    branches = [partial(push, hop_size=2**bit, collective_id=bit) for bit in range(bit_count)]
    mixed, new_weight = lax.switch(step_index % bit_count, branches, state)
    return mixed[None], new_weight


def solution(mesh):
    placed = (
        P("rep", None, "fsdp"),
        P("rep"),
        P(),
        P(None, ("rep", "fsdp"), None),
        P(None, ("rep", "fsdp"), None),
        P(),
    )
    return jax.shard_map(
        on_pairs if mesh.shape["fsdp"] == 2 else on_device,
        mesh=mesh,
        in_specs=placed,
        out_specs=(P("rep", None, "fsdp"), P("rep")),
        check_vma=False,
    )
```

```python
from functools import partial

import jax
import jax.numpy as jnp
from jax import lax
from jax.experimental import pallas as pl
from jax.experimental.pallas import tpu as pltpu
from jax.sharding import PartitionSpec as P

LEARN_RATE = 1.5
EPSILON = 1e-05
PIECES = 4
CHUNK = 256
BLOCK = 512
ROWS = 16
SHARES = (64, 64, 32)
MESH = pl.DeviceIdType.MESH


def shifted(block, axis, distance):
    count = lax.axis_size(axis)
    route = [((i - distance) % count, i) for i in range(count)]
    return lax.ppermute(block, axis, route)


def silu_slope(pre_act):
    sig = jax.nn.sigmoid(pre_act)
    return sig * (1.0 + pre_act * (1.0 - sig))


def normalised(activations, norm_gain):
    wide = activations.astype(jnp.float32)
    mean_square = jnp.mean(wide * wide, axis=-1, keepdims=True)
    return (wide * lax.rsqrt(mean_square + EPSILON) * norm_gain).astype(jnp.bfloat16)


def token_rows(activations, cotangent):
    count = lax.axis_size("fsdp")
    me = lax.axis_index("fsdp")
    width = cotangent.shape[2] // count
    acts, cots = [activations], [lax.dynamic_slice_in_dim(cotangent, me * width, width, 2)]
    for step in range(1, count):
        acts.append(shifted(activations, "fsdp", step))
        theirs = lax.rem(me + step, count)
        cots.append(shifted(lax.dynamic_slice_in_dim(cotangent, theirs * width, width, 2), "fsdp", step))
    return jnp.concatenate(acts, axis=1), jnp.concatenate(cots, axis=1)


def mix(state, hop_size):
    numerator, push_weight, normed, grad_out = state
    depth = numerator.shape[0]
    scale = depth ** (-0.5)
    rows = depth // PIECES
    mixed = []
    partner_weight = shifted(push_weight, "rep", hop_size)
    for start in range(0, depth, rows):
        grad = scale * jnp.einsum(
            "td,th->dh", normed[:, start : start + rows], grad_out, preferred_element_type=jnp.float32
        )
        update = (LEARN_RATE * grad).astype(jnp.bfloat16).astype(jnp.float32)
        local = (numerator[start : start + rows].astype(jnp.float32) - update).astype(jnp.bfloat16)
        theirs = shifted(local, "rep", hop_size)
        mixed.append((0.5 * (local.astype(jnp.float32) + theirs.astype(jnp.float32))).astype(jnp.bfloat16))
    return jnp.concatenate(mixed, axis=0), 0.5 * (push_weight + partner_weight)


def on_device(numerator, push_weight, norm_gain, activations, cotangent, step_index):
    acts, cots = token_rows(activations, cotangent)
    depth, width = numerator.shape[1:]
    scale = depth ** (-0.5)
    normed = normalised(acts, norm_gain).reshape(-1, depth)
    cots = cots.reshape(-1, width)
    eff_weight = (numerator[0].astype(jnp.float32) / push_weight[0]).astype(jnp.bfloat16)
    pre_act = scale * jnp.dot(normed, eff_weight, preferred_element_type=jnp.float32)
    grad_out = (cots.astype(jnp.float32) * silu_slope(pre_act)).astype(jnp.bfloat16)
    bit_count = lax.axis_size("rep").bit_length() - 1
    branches = [partial(mix, hop_size=2**bit) for bit in range(bit_count)]
    mixed, new_weight = lax.switch(
        step_index % bit_count, branches, (numerator[0], push_weight, normed, grad_out)
    )
    return mixed[None], new_weight


def pieces_of(tokens):
    pieces, first = [], 0
    for count in SHARES:
        if first + count < tokens:
            pieces.append((first, count))
            first += count
    return pieces + [(first, tokens - first)]


def push_kernel(
    hop_size, weight_ref, gain_ref, numer_hbm, act_hbm, cot_hbm, mixed_hbm, new_weight_ref,
    act_v, cot_v, normed_v, turned_v, pre_v, grad_v, local_v, theirs_v, weight_v, eff_v,
    load_sem, act_sem, act_send, act_recv, cot_sem, cot_send, cot_recv,
    state_send, state_recv, weight_send, weight_recv, out_sem, go_sem,
):
    rep, col = lax.axis_index("rep"), lax.axis_index("fsdp")
    n_rep = lax.axis_size("rep")
    mate = (rep, 1 - col)
    target = (lax.rem(rep + hop_size, n_rep), col)
    source = (lax.rem(rep + n_rep - hop_size, n_rep), col)
    odd = lax.rem(rep, 2)
    sibling = (rep + 1 - 2 * odd, col)
    leads = odd == (1 if hop_size == 1 else 0)
    tokens, depth = act_hbm.shape
    chunks, _, chunk = local_v.shape
    blocks = depth // BLOCK
    width = chunks * chunk
    scale = depth ** (-0.5)
    pieces = pieces_of(tokens)

    def columns_of(c):
        return pl.ds(pl.multiple_of(c * chunk, chunk), chunk)

    def block_of(k):
        return pl.ds(pl.multiple_of(k * BLOCK, BLOCK), BLOCK)

    def load(c):
        return pltpu.make_async_copy(numer_hbm.at[:, columns_of(c)], local_v.at[c], load_sem.at[c])

    def own_cot(c):
        columns = pl.ds(pl.multiple_of(col * width + c * chunk, chunk), chunk)
        return pltpu.make_async_copy(cot_hbm.at[:, columns], cot_v.at[0, c], cot_sem.at[c])

    def send_cot(c):
        columns = pl.ds(pl.multiple_of((1 - col) * width + c * chunk, chunk), chunk)
        return pltpu.make_async_remote_copy(
            src_ref=cot_hbm.at[:, columns], dst_ref=cot_v.at[1, c],
            send_sem=cot_send.at[c], recv_sem=cot_recv.at[c], device_id=mate, device_id_type=MESH,
        )

    def send_act(i):
        rows = pl.ds(*pieces[i])
        return pltpu.make_async_remote_copy(
            src_ref=act_hbm.at[rows], dst_ref=act_v.at[1, rows],
            send_sem=act_send.at[i], recv_sem=act_recv.at[i], device_id=mate, device_id_type=MESH,
        )

    def send_state(c, k):
        return pltpu.make_async_remote_copy(
            src_ref=local_v.at[c, block_of(k)], dst_ref=theirs_v.at[c, block_of(k)],
            send_sem=state_send.at[c, k], recv_sem=state_recv.at[c, k], device_id=target, device_id_type=MESH,
        )

    def store(c, k):
        return pltpu.make_async_copy(
            theirs_v.at[c, block_of(k)], mixed_hbm.at[block_of(k), columns_of(c)], out_sem.at[c, k]
        )

    def start_sends():
        for i in range(len(pieces)):
            send_act(i).start()
        send_cot(0).start()

    send_weight = pltpu.make_async_remote_copy(
        src_ref=weight_v.at[0], dst_ref=weight_v.at[1],
        send_sem=weight_send, recv_sem=weight_recv, device_id=target, device_id_type=MESH,
    )
    own_act = pltpu.make_async_copy(act_hbm, act_v.at[0], act_sem)

    barrier = pltpu.get_barrier_semaphore()
    for device in (mate, source, sibling):
        pl.semaphore_signal(barrier, inc=1, device_id=device, device_id_type=MESH)
    own_act.start()
    load(0).start()
    own_cot(0).start()
    weight_v[0] = jnp.full(weight_v.shape[1:], weight_ref[0], jnp.float32)
    pl.semaphore_wait(barrier, 3)

    @pl.when(leads)
    def _():
        start_sends()

    send_weight.start()
    for c in range(1, chunks):
        own_cot(c).start()
        load(c).start()

    gain = gain_ref[...].reshape(1, depth)

    def normalise(side, first, count):
        @pl.loop(0, count // ROWS, unroll=True)
        def _(i):
            rows = pl.ds(pl.multiple_of(first + i * ROWS, ROWS), ROWS)
            wide = act_v[side, rows, :].astype(jnp.float32)
            mean_square = jnp.mean(wide * wide, axis=-1, keepdims=True)
            normed = wide * lax.rsqrt(mean_square + EPSILON) * gain
            normed_v[pl.ds(pl.multiple_of(side * tokens + first + i * ROWS, ROWS), ROWS), :] = normed.astype(jnp.bfloat16)

    inverse = 1.0 / weight_v[0, 0:1, :]

    def weigh(c):
        @pl.loop(0, blocks)
        def _(k):
            eff_v[block_of(k), :] = (local_v[c, block_of(k), :].astype(jnp.float32) * inverse).astype(jnp.bfloat16)

    def forward(first, count):
        rows = pl.ds(first, count)
        pre_v[rows, :] = jnp.dot(normed_v[rows, :], eff_v[...], preferred_element_type=jnp.float32)

    def slopes(c, side):
        rows = pl.ds(side * tokens, tokens)
        grad_v[rows, :] = (
            cot_v[side, c].astype(jnp.float32) * silu_slope(scale * pre_v[rows, :])
        ).astype(jnp.bfloat16)

    def turn(side, k):
        turned_v[side, block_of(k), :] = normed_v[pl.ds(side * tokens, tokens), block_of(k)].T

    def backward(c, first=False):
        @pl.loop(0, blocks, unroll=True)
        def _(k):
            if first:
                turn(0, k)
                turn(1, k)
            grad = sum(
                jnp.dot(
                    turned_v[side, block_of(k), :], grad_v[pl.ds(side * tokens, tokens), :],
                    preferred_element_type=jnp.float32,
                )
                for side in range(2)
            )
            update = (LEARN_RATE * (scale * grad)).astype(jnp.bfloat16).astype(jnp.float32)
            local_v[c, block_of(k), :] = (local_v[c, block_of(k), :].astype(jnp.float32) - update).astype(jnp.bfloat16)
            send_state(c, k).start()

    own_act.wait()
    normalise(0, 0, tokens)
    load(0).wait()
    weigh(0)
    forward(0, tokens)
    own_cot(0).wait()
    slopes(0, 0)

    @pl.when(jnp.logical_not(leads))
    def _():
        pl.semaphore_wait(go_sem, 1)
        start_sends()

    for i in range(len(pieces)):
        send_act(i).wait_recv()
        normalise(1, *pieces[i])
        if i == len(pieces) - 2:
            forward(tokens, sum(pieces[i]))
    forward(tokens + pieces[-1][0], pieces[-1][1])
    send_cot(0).wait_recv()
    for c in range(1, chunks):
        send_cot(c).start()

    @pl.when(leads)
    def _():
        pl.semaphore_signal(go_sem, inc=1, device_id=sibling, device_id_type=MESH)

    slopes(0, 1)

    backward(0, first=True)

    @pl.loop(1, chunks)
    def _(c):
        load(c).wait()
        weigh(c)
        forward(0, 2 * tokens)
        own_cot(c).wait()
        slopes(c, 0)
        send_cot(c).wait_recv()
        slopes(c, 1)
        backward(c)

    send_weight.wait_recv()
    new_weight_ref[0] = jnp.max(0.5 * (weight_v[0] + weight_v[1]))

    @pl.loop(0, chunks)
    def _(c):
        @pl.loop(0, blocks)
        def _(k):
            send_state(c, k).wait_recv()
            both = local_v[c, block_of(k), :].astype(jnp.float32) + theirs_v[c, block_of(k), :].astype(jnp.float32)
            theirs_v[c, block_of(k), :] = (0.5 * both).astype(jnp.bfloat16)
            store(c, k).start()

    for i in range(len(pieces)):
        send_act(i).wait_send()
    send_weight.wait_send()

    @pl.loop(0, chunks)
    def _(c):
        send_cot(c).wait_send()

        @pl.loop(0, blocks)
        def _(k):
            send_state(c, k).wait_send()
            store(c, k).wait()


def push(state, hop_size, collective_id):
    numerator, push_weight, norm_gain, activations, cotangent = state
    depth, width = numerator.shape
    tokens = activations.shape[0]
    chunks, blocks = width // CHUNK, depth // BLOCK
    vmem, hbm = pl.BlockSpec(memory_space=pltpu.VMEM), pl.BlockSpec(memory_space=pl.ANY)
    smem = pl.BlockSpec(memory_space=pltpu.SMEM)
    dma = pltpu.SemaphoreType.DMA
    arrivals = len(pieces_of(tokens))
    return pl.pallas_call(
        partial(push_kernel, hop_size),
        out_shape=(
            jax.ShapeDtypeStruct((depth, width), jnp.bfloat16),
            jax.ShapeDtypeStruct((1,), jnp.float32),
        ),
        in_specs=[smem, vmem, hbm, hbm, hbm],
        out_specs=(hbm, smem),
        scratch_shapes=[
            pltpu.VMEM((2, tokens, depth), jnp.bfloat16),
            pltpu.VMEM((2, chunks, tokens, CHUNK), jnp.bfloat16),
            pltpu.VMEM((2 * tokens, depth), jnp.bfloat16),
            pltpu.VMEM((2, depth, tokens), jnp.bfloat16),
            pltpu.VMEM((2 * tokens, CHUNK), jnp.float32),
            pltpu.VMEM((2 * tokens, CHUNK), jnp.bfloat16),
            pltpu.VMEM((chunks, depth, CHUNK), jnp.bfloat16),
            pltpu.VMEM((chunks, depth, CHUNK), jnp.bfloat16),
            pltpu.VMEM((2, 8, CHUNK), jnp.float32),
            pltpu.VMEM((depth, CHUNK), jnp.bfloat16),
            dma((chunks,)), dma, dma((arrivals,)), dma((arrivals,)), dma((chunks,)), dma((chunks,)), dma((chunks,)),
            dma((chunks, blocks)), dma((chunks, blocks)), dma, dma, dma((chunks, blocks)),
            pltpu.SemaphoreType.REGULAR,
        ],
        compiler_params=pltpu.CompilerParams(
            collective_id=collective_id, has_side_effects=True, vmem_limit_bytes=48 * 2**20
        ),
        cost_estimate=pl.CostEstimate(
            flops=8 * tokens * depth * width, bytes_accessed=4 * depth * width, transcendentals=2 * tokens * width
        ),
    )(push_weight, norm_gain, numerator, activations, cotangent)


def on_pairs(numerator, push_weight, norm_gain, activations, cotangent, step_index):
    depth = numerator.shape[1]
    state = (
        numerator[0], push_weight, norm_gain,
        activations.reshape(-1, depth), cotangent.reshape(-1, cotangent.shape[2]),
    )
    bit_count = lax.axis_size("rep").bit_length() - 1
    branches = [partial(push, hop_size=2**bit, collective_id=bit) for bit in range(bit_count)]
    mixed, new_weight = lax.switch(step_index % bit_count, branches, state)
    return mixed[None], new_weight


def solution(mesh):
    placed = (
        P("rep", None, "fsdp"),
        P("rep"),
        P(),
        P(None, ("rep", "fsdp"), None),
        P(None, ("rep", "fsdp"), None),
        P(),
    )
    return jax.shard_map(
        on_pairs if mesh.shape["fsdp"] == 2 else on_device,
        mesh=mesh,
        in_specs=placed,
        out_specs=(P("rep", None, "fsdp"), P("rep")),
        check_vma=False,
    )
```

```python
from functools import partial

import jax
import jax.numpy as jnp
from jax import lax
from jax.experimental import pallas as pl
from jax.experimental.pallas import tpu as pltpu
from jax.sharding import PartitionSpec as P

LEARN_RATE = 1.5
EPSILON = 1e-05
PIECES = 4
CHUNK = 256
BLOCK = 256
ROWS = 16
SHARES = (64, 64, 32)
MESH = pl.DeviceIdType.MESH


def shifted(block, axis, distance):
    count = lax.axis_size(axis)
    route = [((i - distance) % count, i) for i in range(count)]
    return lax.ppermute(block, axis, route)


def silu_slope(pre_act):
    sig = jax.nn.sigmoid(pre_act)
    return sig * (1.0 + pre_act * (1.0 - sig))


def normalised(activations, norm_gain):
    wide = activations.astype(jnp.float32)
    mean_square = jnp.mean(wide * wide, axis=-1, keepdims=True)
    return (wide * lax.rsqrt(mean_square + EPSILON) * norm_gain).astype(jnp.bfloat16)


def token_rows(activations, cotangent):
    count = lax.axis_size("fsdp")
    me = lax.axis_index("fsdp")
    width = cotangent.shape[2] // count
    acts, cots = [activations], [lax.dynamic_slice_in_dim(cotangent, me * width, width, 2)]
    for step in range(1, count):
        acts.append(shifted(activations, "fsdp", step))
        theirs = lax.rem(me + step, count)
        cots.append(shifted(lax.dynamic_slice_in_dim(cotangent, theirs * width, width, 2), "fsdp", step))
    return jnp.concatenate(acts, axis=1), jnp.concatenate(cots, axis=1)


def mix(state, hop_size):
    numerator, push_weight, normed, grad_out = state
    depth = numerator.shape[0]
    scale = depth ** (-0.5)
    rows = depth // PIECES
    mixed = []
    partner_weight = shifted(push_weight, "rep", hop_size)
    for start in range(0, depth, rows):
        grad = scale * jnp.einsum(
            "td,th->dh", normed[:, start : start + rows], grad_out, preferred_element_type=jnp.float32
        )
        update = (LEARN_RATE * grad).astype(jnp.bfloat16).astype(jnp.float32)
        local = (numerator[start : start + rows].astype(jnp.float32) - update).astype(jnp.bfloat16)
        theirs = shifted(local, "rep", hop_size)
        mixed.append((0.5 * (local.astype(jnp.float32) + theirs.astype(jnp.float32))).astype(jnp.bfloat16))
    return jnp.concatenate(mixed, axis=0), 0.5 * (push_weight + partner_weight)


def on_device(numerator, push_weight, norm_gain, activations, cotangent, step_index):
    acts, cots = token_rows(activations, cotangent)
    depth, width = numerator.shape[1:]
    scale = depth ** (-0.5)
    normed = normalised(acts, norm_gain).reshape(-1, depth)
    cots = cots.reshape(-1, width)
    eff_weight = (numerator[0].astype(jnp.float32) / push_weight[0]).astype(jnp.bfloat16)
    pre_act = scale * jnp.dot(normed, eff_weight, preferred_element_type=jnp.float32)
    grad_out = (cots.astype(jnp.float32) * silu_slope(pre_act)).astype(jnp.bfloat16)
    bit_count = lax.axis_size("rep").bit_length() - 1
    branches = [partial(mix, hop_size=2**bit) for bit in range(bit_count)]
    mixed, new_weight = lax.switch(
        step_index % bit_count, branches, (numerator[0], push_weight, normed, grad_out)
    )
    return mixed[None], new_weight


def pieces_of(tokens):
    pieces, first = [], 0
    for count in SHARES:
        if first + count < tokens:
            pieces.append((first, count))
            first += count
    return pieces + [(first, tokens - first)]


def push_kernel(
    hop_size, weight_ref, gain_ref, numer_hbm, act_hbm, cot_hbm, mixed_hbm, new_weight_ref,
    act_v, cot_v, normed_v, turned_v, pre_v, grad_v, local_v, theirs_v, weight_v, eff_v,
    load_sem, act_sem, act_send, act_recv, cot_sem, cot_send, cot_recv,
    state_send, state_recv, weight_send, weight_recv, out_sem, go_sem,
):
    rep, col = lax.axis_index("rep"), lax.axis_index("fsdp")
    n_rep = lax.axis_size("rep")
    mate = (rep, 1 - col)
    target = (lax.rem(rep + hop_size, n_rep), col)
    source = (lax.rem(rep + n_rep - hop_size, n_rep), col)
    odd = lax.rem(rep, 2)
    sibling = (rep + 1 - 2 * odd, col)
    leads = odd == (1 if hop_size == 1 else 0)
    tokens, depth = act_hbm.shape
    chunks, _, chunk = local_v.shape
    blocks = depth // BLOCK
    width = chunks * chunk
    scale = depth ** (-0.5)
    pieces = pieces_of(tokens)

    def columns_of(c):
        return pl.ds(pl.multiple_of(c * chunk, chunk), chunk)

    def block_of(k):
        return pl.ds(pl.multiple_of(k * BLOCK, BLOCK), BLOCK)

    def load(c):
        return pltpu.make_async_copy(numer_hbm.at[:, columns_of(c)], local_v.at[c], load_sem.at[c])

    def own_cot(c):
        columns = pl.ds(pl.multiple_of(col * width + c * chunk, chunk), chunk)
        return pltpu.make_async_copy(cot_hbm.at[:, columns], cot_v.at[0, c], cot_sem.at[c])

    def send_cot(c):
        columns = pl.ds(pl.multiple_of((1 - col) * width + c * chunk, chunk), chunk)
        return pltpu.make_async_remote_copy(
            src_ref=cot_hbm.at[:, columns], dst_ref=cot_v.at[1, c],
            send_sem=cot_send.at[c], recv_sem=cot_recv.at[c], device_id=mate, device_id_type=MESH,
        )

    def send_act(i):
        rows = pl.ds(*pieces[i])
        return pltpu.make_async_remote_copy(
            src_ref=act_hbm.at[rows], dst_ref=act_v.at[1, rows],
            send_sem=act_send.at[i], recv_sem=act_recv.at[i], device_id=mate, device_id_type=MESH,
        )

    def send_state(c, k):
        return pltpu.make_async_remote_copy(
            src_ref=local_v.at[c, block_of(k)], dst_ref=theirs_v.at[c, block_of(k)],
            send_sem=state_send.at[c, k], recv_sem=state_recv.at[c, k], device_id=target, device_id_type=MESH,
        )

    def store(c, k):
        return pltpu.make_async_copy(
            theirs_v.at[c, block_of(k)], mixed_hbm.at[block_of(k), columns_of(c)], out_sem.at[c, k]
        )

    def start_sends():
        for i in range(len(pieces)):
            send_act(i).start()
        send_cot(0).start()

    send_weight = pltpu.make_async_remote_copy(
        src_ref=weight_v.at[0], dst_ref=weight_v.at[1],
        send_sem=weight_send, recv_sem=weight_recv, device_id=target, device_id_type=MESH,
    )
    own_act = pltpu.make_async_copy(act_hbm, act_v.at[0], act_sem)

    barrier = pltpu.get_barrier_semaphore()
    for device in (mate, source, sibling):
        pl.semaphore_signal(barrier, inc=1, device_id=device, device_id_type=MESH)
    own_act.start()
    load(0).start()
    own_cot(0).start()
    weight_v[0] = jnp.full(weight_v.shape[1:], weight_ref[0], jnp.float32)
    pl.semaphore_wait(barrier, 3)

    @pl.when(leads)
    def _():
        start_sends()

    send_weight.start()
    for c in range(1, chunks):
        own_cot(c).start()
        load(c).start()

    gain = gain_ref[...].reshape(1, depth)

    def normalise(side, first, count):
        @pl.loop(0, count // ROWS, unroll=True)
        def _(i):
            rows = pl.ds(pl.multiple_of(first + i * ROWS, ROWS), ROWS)
            wide = act_v[side, rows, :].astype(jnp.float32)
            mean_square = jnp.mean(wide * wide, axis=-1, keepdims=True)
            normed = wide * lax.rsqrt(mean_square + EPSILON) * gain
            normed_v[pl.ds(pl.multiple_of(side * tokens + first + i * ROWS, ROWS), ROWS), :] = normed.astype(jnp.bfloat16)

    inverse = 1.0 / weight_v[0, 0:1, :]

    def weigh(c):
        @pl.loop(0, blocks)
        def _(k):
            eff_v[block_of(k), :] = (local_v[c, block_of(k), :].astype(jnp.float32) * inverse).astype(jnp.bfloat16)

    def forward(first, count):
        rows = pl.ds(first, count)
        pre_v[rows, :] = jnp.dot(normed_v[rows, :], eff_v[...], preferred_element_type=jnp.float32)

    def slopes(c, side):
        rows = pl.ds(side * tokens, tokens)
        grad_v[rows, :] = (
            cot_v[side, c].astype(jnp.float32) * silu_slope(scale * pre_v[rows, :])
        ).astype(jnp.bfloat16)

    def turn(side, k):
        turned_v[side, block_of(k), :] = normed_v[pl.ds(side * tokens, tokens), block_of(k)].T

    def backward(c, first=False):
        @pl.loop(0, blocks, unroll=True)
        def _(k):
            if first:

                @pl.when(k > 0)
                def _():
                    turn(0, k)

                turn(1, k)
            grad = sum(
                jnp.dot(
                    turned_v[side, block_of(k), :], grad_v[pl.ds(side * tokens, tokens), :],
                    preferred_element_type=jnp.float32,
                )
                for side in range(2)
            )
            update = (LEARN_RATE * (scale * grad)).astype(jnp.bfloat16).astype(jnp.float32)
            local_v[c, block_of(k), :] = (local_v[c, block_of(k), :].astype(jnp.float32) - update).astype(jnp.bfloat16)
            send_state(c, k).start()

    own_act.wait()
    normalise(0, 0, tokens)
    load(0).wait()
    weigh(0)
    forward(0, tokens)
    own_cot(0).wait()
    slopes(0, 0)
    turn(0, 0)

    @pl.when(jnp.logical_not(leads))
    def _():
        pl.semaphore_wait(go_sem, 1)
        start_sends()

    for i in range(len(pieces)):
        send_act(i).wait_recv()
        normalise(1, *pieces[i])
        if i == len(pieces) - 2:

            @pl.when(leads)
            def _():
                pl.semaphore_signal(go_sem, inc=1, device_id=sibling, device_id_type=MESH)

            forward(tokens, sum(pieces[i]))
    forward(tokens + pieces[-1][0], pieces[-1][1])
    send_cot(0).wait_recv()
    for c in range(1, chunks):
        send_cot(c).start()

    slopes(0, 1)

    backward(0, first=True)

    @pl.loop(1, chunks)
    def _(c):
        load(c).wait()
        weigh(c)
        forward(0, 2 * tokens)
        own_cot(c).wait()
        slopes(c, 0)
        send_cot(c).wait_recv()
        slopes(c, 1)
        backward(c)

    send_weight.wait_recv()
    new_weight_ref[0] = jnp.max(0.5 * (weight_v[0] + weight_v[1]))

    @pl.loop(0, chunks)
    def _(c):
        @pl.loop(0, blocks)
        def _(k):
            send_state(c, k).wait_recv()
            both = local_v[c, block_of(k), :].astype(jnp.float32) + theirs_v[c, block_of(k), :].astype(jnp.float32)
            theirs_v[c, block_of(k), :] = (0.5 * both).astype(jnp.bfloat16)
            store(c, k).start()

    for i in range(len(pieces)):
        send_act(i).wait_send()
    send_weight.wait_send()

    @pl.loop(0, chunks)
    def _(c):
        send_cot(c).wait_send()

        @pl.loop(0, blocks)
        def _(k):
            send_state(c, k).wait_send()
            store(c, k).wait()


def push(state, hop_size, collective_id):
    numerator, push_weight, norm_gain, activations, cotangent = state
    depth, width = numerator.shape
    tokens = activations.shape[0]
    chunks, blocks = width // CHUNK, depth // BLOCK
    vmem, hbm = pl.BlockSpec(memory_space=pltpu.VMEM), pl.BlockSpec(memory_space=pl.ANY)
    smem = pl.BlockSpec(memory_space=pltpu.SMEM)
    dma = pltpu.SemaphoreType.DMA
    arrivals = len(pieces_of(tokens))
    return pl.pallas_call(
        partial(push_kernel, hop_size),
        out_shape=(
            jax.ShapeDtypeStruct((depth, width), jnp.bfloat16),
            jax.ShapeDtypeStruct((1,), jnp.float32),
        ),
        in_specs=[smem, vmem, hbm, hbm, hbm],
        out_specs=(hbm, smem),
        scratch_shapes=[
            pltpu.VMEM((2, tokens, depth), jnp.bfloat16),
            pltpu.VMEM((2, chunks, tokens, CHUNK), jnp.bfloat16),
            pltpu.VMEM((2 * tokens, depth), jnp.bfloat16),
            pltpu.VMEM((2, depth, tokens), jnp.bfloat16),
            pltpu.VMEM((2 * tokens, CHUNK), jnp.float32),
            pltpu.VMEM((2 * tokens, CHUNK), jnp.bfloat16),
            pltpu.VMEM((chunks, depth, CHUNK), jnp.bfloat16),
            pltpu.VMEM((chunks, depth, CHUNK), jnp.bfloat16),
            pltpu.VMEM((2, 8, CHUNK), jnp.float32),
            pltpu.VMEM((depth, CHUNK), jnp.bfloat16),
            dma((chunks,)), dma, dma((arrivals,)), dma((arrivals,)), dma((chunks,)), dma((chunks,)), dma((chunks,)),
            dma((chunks, blocks)), dma((chunks, blocks)), dma, dma, dma((chunks, blocks)),
            pltpu.SemaphoreType.REGULAR,
        ],
        compiler_params=pltpu.CompilerParams(
            collective_id=collective_id, has_side_effects=True, vmem_limit_bytes=48 * 2**20
        ),
        cost_estimate=pl.CostEstimate(
            flops=8 * tokens * depth * width, bytes_accessed=4 * depth * width, transcendentals=2 * tokens * width
        ),
    )(push_weight, norm_gain, numerator, activations, cotangent)


def on_pairs(numerator, push_weight, norm_gain, activations, cotangent, step_index):
    depth = numerator.shape[1]
    state = (
        numerator[0], push_weight, norm_gain,
        activations.reshape(-1, depth), cotangent.reshape(-1, cotangent.shape[2]),
    )
    bit_count = lax.axis_size("rep").bit_length() - 1
    branches = [partial(push, hop_size=2**bit, collective_id=bit) for bit in range(bit_count)]
    mixed, new_weight = lax.switch(step_index % bit_count, branches, state)
    return mixed[None], new_weight


def solution(mesh):
    placed = (
        P("rep", None, "fsdp"),
        P("rep"),
        P(),
        P(None, ("rep", "fsdp"), None),
        P(None, ("rep", "fsdp"), None),
        P(),
    )
    return jax.shard_map(
        on_pairs if mesh.shape["fsdp"] == 2 else on_device,
        mesh=mesh,
        in_specs=placed,
        out_specs=(P("rep", None, "fsdp"), P("rep")),
        check_vma=False,
    )
```
